128 devices in a mesh: row: 16 (over z, y), col: 8 (over x, core).
Axes of the slice: x: 4, y: 4, z: 4, core: 2. Of those that a mesh axis runs over, the one named last changes fastest.
Arguments:
- points: bfloat16 [24576, 256], P(('row', 'col')), may hold values from -0.5 to 0.5
- lengthscale: float32 [256], replicated, may hold values from 0.1 to 4
- solution_vals: float32 [24576], P(('row', 'col')), may hold values from -6 to 6
- solution_grads: float32 [24576, 256], P(('row', 'col')), may hold values from -6 to 6
- residual_vals: float32 [24576], P(('row', 'col')), may hold values from -80 to 80
- residual_grads: float32 [24576, 256], P(('row', 'col')), may hold values from -80 to 80
- direction_vals: float32 [24576], P(('row', 'col')), may hold values from -80 to 80
- direction_grads: float32 [24576, 256], P(('row', 'col')), may hold values from -80 to 80
Outputs:
- next_solution_vals: float32 [24576], P(('row', 'col'))
- next_solution_grads: float32 [24576, 256], P(('row', 'col'))
- next_residual_vals: float32 [24576], P(('row', 'col'))
- next_residual_grads: float32 [24576, 256], P(('row', 'col'))
- next_direction_vals: float32 [24576], P(('row', 'col'))
- next_direction_grads: float32 [24576, 256], P(('row', 'col'))
The draws below stay inside these ranges and needn't reach their ends.
All inputs are finite; a program needn't handle non-finite values.
Results may differ from the reference program's by a relative error of at most 0.0038.
Values may be sent and summed in bfloat16 or wider, within the bound.
A program may use at most 64 MiB of HBM per device.

```python
import math
import jax
import jax.numpy as jnp
from jax import lax

D = 256
NPTS = 24576


def rising(count, span):
    return span ** (jnp.arange(count, dtype=jnp.float32) / (count - 1))


def column_scale(key, width):
    return 10.0 ** jax.random.uniform(key, (width,), jnp.float32, -1.0, 0.0)


def draw_residual_vals(key, part):
    key = jax.random.fold_in(key, 11)
    noise = jnp.clip(jax.random.normal(key, (NPTS,), jnp.float32), -5.0, 5.0)
    span = 10.0
    return noise * rising(NPTS, span)


def draw_residual_grads(key, part):
    key = jax.random.fold_in(key, 12)
    first_key, second_key = jax.random.split(key)
    noise = jnp.clip(jax.random.normal(first_key, (NPTS, D), jnp.float32), -5.0, 5.0)
    span = 10.0
    return noise * rising(NPTS, span)[:, None] * column_scale(second_key, D)[None, :]


def draw_direction_vals(key, part):
    key = jax.random.fold_in(key, 13)
    noise = jnp.clip(jax.random.normal(key, (NPTS,), jnp.float32), -5.0, 5.0)
    span = 10.0
    return noise * rising(NPTS, span)


def draw_direction_grads(key, part):
    key = jax.random.fold_in(key, 14)
    first_key, second_key = jax.random.split(key)
    noise = jnp.clip(jax.random.normal(first_key, (NPTS, D), jnp.float32), -5.0, 5.0)
    span = 10.0
    return noise * rising(NPTS, span)[:, None] * column_scale(second_key, D)[None, :]


def block_scale(key, dims, pieces, smallest, largest):
    def one(axis_at, blocks):
        heights = jax.random.uniform(jax.random.fold_in(jax.random.fold_in(key, 6), axis_at), (blocks,), jnp.float32, smallest / len(pieces), largest / len(pieces))
        return jnp.repeat(jnp.exp(heights), dims[axis_at] // blocks).reshape((-1,) + (1,) * (len(dims) - axis_at - 1))

    loudness = one(*pieces[0])
    for cut in pieces[1:]:
        loudness = loudness * one(*cut)
    return loudness


def centred(rng, dims, spread, most, cuts=(), held_as=jnp.bfloat16):
    values = jax.random.normal(rng, dims, jnp.float32) * spread
    if len(cuts) > 0:
        values = block_scale(rng, dims, cuts, -0.22, 0.18) * values
    return jnp.clip(values, min=-most, max=most).astype(held_as)


def setup_inputs(seed: int = 0) -> dict:
    keys = jax.random.split(jax.random.key(seed), 9)
    points = centred(keys[0], (NPTS, D), 0.125, 0.5, ((0, 128),))
    lengthscale = jnp.clip(jnp.exp(jax.random.uniform(keys[1], (D,), jnp.float32, math.log(0.1), math.log(4.0))), 0.1, 4.0)
    solution_vals = centred(keys[2], (NPTS,), 1.0, 6.0, ((0, 128),), jnp.float32)
    solution_grads = centred(keys[3], (NPTS, D), 1.0, 6.0, ((0, 128),), jnp.float32)
    residual_vals = draw_residual_vals(jax.random.fold_in(keys[8], 71), 0)
    residual_grads = draw_residual_grads(jax.random.fold_in(keys[8], 71), 0)
    direction_vals = draw_direction_vals(jax.random.fold_in(keys[8], 71), 0)
    direction_grads = draw_direction_grads(jax.random.fold_in(keys[8], 71), 0)
    return {"points": points, "lengthscale": lengthscale, "solution_vals": solution_vals, "solution_grads": solution_grads, "residual_vals": residual_vals, "residual_grads": residual_grads, "direction_vals": direction_vals, "direction_grads": direction_grads}


nugget_level = 4.0

def contract(left, right):
    return lax.dot_general(left, right, (((1,), (1,)), ((), ())), preferred_element_type=jnp.float32)

def partial_terms(target_points, source_points, source_vals, source_grads):
    source_square = lax.optimization_barrier(jnp.sum(jnp.square(source_points.astype(jnp.float32)), axis=1))
    source_shift = lax.optimization_barrier(jnp.sum(source_points.astype(jnp.float32) * source_grads.astype(jnp.float32), axis=1))
    source_level = source_vals.astype(jnp.float32)
    row_count, width = target_points.shape
    block_size = math.gcd(row_count, 1024)

    def one_block(target_tile):
        target_square = lax.optimization_barrier(jnp.sum(jnp.square(target_tile.astype(jnp.float32)), axis=1))
        distance = target_square[:, None] + source_square[None, :] - 2.0 * contract(target_tile, source_points)
        kernel = jnp.exp(-0.5 * distance)
        inner_terms = contract(target_tile, source_grads) - source_shift[None, :]
        weight = kernel * (source_level[None, :] + inner_terms)
        total_weight = lax.optimization_barrier(jnp.sum(weight, axis=1))
        mixed_terms = jnp.dot(kernel.astype(jnp.bfloat16), source_grads, preferred_element_type=jnp.float32)
        mixed_terms = mixed_terms + jnp.dot(weight.astype(jnp.bfloat16), source_points, preferred_element_type=jnp.float32)
        return (total_weight, mixed_terms)
    tiles = target_points.reshape(row_count // block_size, block_size, width)
    total_weight, mixed_terms = lax.map(one_block, tiles)
    return (total_weight.reshape(row_count), mixed_terms.reshape(row_count, width))

def reference(points, lengthscale, solution_vals, solution_grads, residual_vals, residual_grads, direction_vals, direction_grads):
    root_scale = jnp.sqrt(lengthscale)
    scaled = (points.astype(jnp.float32) * root_scale).astype(jnp.bfloat16)
    level_low = direction_vals.astype(jnp.bfloat16)
    slope_low = (direction_grads * root_scale).astype(jnp.bfloat16)
    total_weight, mixed_terms = partial_terms(scaled, scaled, level_low, slope_low)
    image_vals = total_weight + nugget_level * direction_vals
    image_grads = root_scale * (mixed_terms - scaled.astype(jnp.float32) * total_weight[:, None]) + nugget_level * direction_grads
    norm_now = jnp.sum(residual_vals * residual_vals) + jnp.sum(residual_grads * residual_grads)
    curvature = jnp.sum(direction_vals * image_vals) + jnp.sum(direction_grads * image_grads)
    step_size = norm_now / curvature
    next_solution_vals = solution_vals + step_size * direction_vals
    next_solution_grads = solution_grads + step_size * direction_grads
    next_residual_vals = residual_vals - step_size * image_vals
    next_residual_grads = residual_grads - step_size * image_grads
    norm_next = jnp.sum(next_residual_vals * next_residual_vals) + jnp.sum(next_residual_grads * next_residual_grads)
    ratio_next = norm_next / norm_now
    next_direction_vals = next_residual_vals + ratio_next * direction_vals
    next_direction_grads = next_residual_grads + ratio_next * direction_grads
    return (next_solution_vals, next_solution_grads, next_residual_vals, next_residual_grads, next_direction_vals, next_direction_grads)
```

```python
import functools
import math

import jax
import jax.numpy as jnp
from jax import lax
from jax.experimental import pallas as pl
from jax.experimental.pallas import tpu as pltpu
from jax.sharding import PartitionSpec as P

MESH = pl.DeviceIdType.MESH
LOG2E = math.log2(math.e)
NUGGET = 4.0
RING = 4
ROWS = 192
DIM = 256
LANES = 128
TAIL = ROWS - LANES
X_ROWS = 2 * ROWS
S_ROWS = 2 * ROWS
V_ROWS = 16
BLOCK = X_ROWS + S_ROWS + V_ROWS
CUT = X_ROWS
OFFSETS = (0, 1, 3, 2)
COUNT = 128


def slot_of(f, s):
    fi, si = OFFSETS.index(f % RING), OFFSETS.index(s % RING)
    return fi if si == 0 else 4 + 3 * fi + si - 1


def target_slot(t, k):
    return 2 * OFFSETS.index(t % RING) + k


def kernel(
    points_ref,
    scale_ref,
    sv_ref,
    sg_ref,
    rv_ref,
    rg_ref,
    dv_ref,
    dg_ref,
    nsv_ref,
    nsg_ref,
    nrv_ref,
    nrg_ref,
    ndv_ref,
    ndg_ref,
    slots,
    tx,
    ta,
    acc,
    tot,
    part,
    ptot,
    rsb,
    rst,
    vecs,
    mine,
    arb,
    g_send,
    g_recv,
    x_send,
    x_recv,
    r_send,
    r_recv,
    p_send,
    p_recv,
    a_send,
    a_recv,
):
    row, col = lax.axis_index("row"), lax.axis_index("col")
    z, y = row // RING, row % RING
    x, c = col // 2, col % 2
    o = 1 - c

    def first(d):
        return (z * RING + (y + d) % RING, col)

    def second(d, core):
        return (((z + o * d) % RING) * RING + y, ((x + c * d) % RING) * 2 + core)

    def third(d, core):
        return (((z + c * d) % RING) * RING + y, ((x + o * d) % RING) * 2 + core)

    barrier = pltpu.get_barrier_semaphore()
    near = [first(1), first(3), second(1, c), second(3, c)]
    near += [third(t, c) for t in (1, 2, 3)] + [third(t, o) for t in range(RING)]
    near += [second(t, o) for t in (1, 2, 3)]
    for peer in near:
        pl.semaphore_signal(barrier, inc=1, device_id=peer, device_id_type=MESH)

    root = jnp.sqrt(scale_ref[...])
    scaled = (points_ref[...].astype(jnp.float32) * root).astype(jnp.bfloat16)
    slope = (dg_ref[...] * root).astype(jnp.bfloat16)
    for p in range(2):
        lanes = slice(p * LANES, (p + 1) * LANES)
        slots[0, p * ROWS : (p + 1) * ROWS, :] = scaled[:, lanes]
        slots[0, X_ROWS + p * ROWS : X_ROWS + (p + 1) * ROWS, :] = slope[:, lanes]
        tx[0, p * ROWS : (p + 1) * ROWS, :] = scaled[:, lanes]
    wide = scaled.astype(jnp.float32)
    square = jnp.sum(wide * wide, axis=1, keepdims=True)
    shift = jnp.sum(wide * slope.astype(jnp.float32), axis=1, keepdims=True)
    lane = lax.broadcasted_iota(jnp.int32, (ROWS, LANES), 1)
    both = jnp.where(lane == 0, square, jnp.where(lane == 1, shift, 0.0))
    both = jnp.concatenate([both, both[LANES:]], axis=0)
    across = both.T
    level = dv_ref[...].astype(jnp.bfloat16).astype(jnp.float32)
    base = across[0:1] * (-0.5 * LOG2E)
    terms = (
        base[:, :LANES],
        base[:, LANES:],
        level[:, :LANES] - across[1:2, :LANES],
        jnp.concatenate([level[:, LANES:], level[:, LANES:]], axis=1) - across[1:2, LANES:],
    )
    vecs[...] = jnp.zeros_like(vecs)
    for i, term in enumerate(terms):
        for j in range(3):
            piece = term.astype(jnp.bfloat16).astype(jnp.float32)
            vecs[3 * i + j : 3 * i + j + 1, :] = piece
            term = term - piece
    slots[0, X_ROWS + S_ROWS :, :] = vecs[...].astype(jnp.bfloat16)

    copies = {}

    def describe(f, s, half, source, peer):
        n = len(copies)
        where = {None: slice(0, BLOCK), 0: slice(0, CUT), 1: slice(CUT, BLOCK)}[half]
        rows = pl.ds(where.start, where.stop - where.start)
        copies[f, s, half] = pltpu.make_async_remote_copy(
            src_ref=slots.at[slot_of(*source), rows],
            dst_ref=slots.at[slot_of(f, s), rows],
            send_sem=g_send.at[n],
            recv_sem=g_recv.at[n],
            device_id=peer,
            device_id_type=MESH,
        )

    describe(1, 0, None, (0, 0), first(3))
    describe(3, 0, None, (0, 0), first(1))
    describe(2, 0, 0, (3, 0), first(1))
    describe(2, 0, 1, (1, 0), first(3))
    for f in OFFSETS:
        describe(f, 1, None, (f, 0), second(3, c))
        describe(f, 3, None, (f, 0), second(1, c))
        describe(f, 2, 0, (f, 3), second(1, c))
        describe(f, 2, 1, (f, 1), second(3, c))

    x_copies, r_copies, p_copies = {}, {}, {}
    for t in OFFSETS:
        for k in range(2):
            if (t, k) == (0, 0):
                continue
            n = target_slot(t, k)
            back = (RING - t) % RING
            x_copies[t, k] = pltpu.make_async_remote_copy(
                src_ref=slots.at[0, pl.ds(0, X_ROWS)],
                dst_ref=tx.at[n],
                send_sem=x_send.at[n],
                recv_sem=x_recv.at[n],
                device_id=second(back, o) if k else third(back, c),
                device_id_type=MESH,
            )
            owner = third(back, o) if k else third(back, c)
            r_copies[t, k] = pltpu.make_async_remote_copy(
                src_ref=part.at[target_slot(back, k)],
                dst_ref=rsb.at[n],
                send_sem=r_send.at[n],
                recv_sem=r_recv.at[n],
                device_id=owner,
                device_id_type=MESH,
            )
            p_copies[t, k] = pltpu.make_async_remote_copy(
                src_ref=ptot.at[target_slot(back, k)],
                dst_ref=rst.at[n],
                send_sem=p_send.at[n],
                recv_sem=p_recv.at[n],
                device_id=owner,
                device_id_type=MESH,
            )

    def tile_points(i):
        planes = []
        for p in range(2):
            rows = slice(p * ROWS, (p + 1) * ROWS)
            planes.append(jnp.concatenate([tx[2 * i, rows, :], tx[2 * i + 1, rows, :]], axis=0))
        return jnp.concatenate(planes, axis=1)

    def target_base(i):
        value = tile_points(i).astype(jnp.float32)
        total = jnp.sum(value * value, axis=1, keepdims=True) * (-0.5 * LOG2E)
        ta[i] = jnp.broadcast_to(total, (2 * ROWS, LANES))

    low = lax.broadcasted_iota(jnp.int32, (1, LANES), 1) < TAIL

    def sources(g):
        held = range(4 * g, 4 * g + 4)

        def plane(p):
            top = p * ROWS
            pieces = [slots[s, top : top + LANES, :] for s in held]
            pieces += [slots[s, top + LANES : top + ROWS, :] for s in held]
            return jnp.concatenate(pieces, axis=0)

        xs = jnp.concatenate([plane(0), plane(1)], axis=1)
        ss = jnp.concatenate([plane(2), plane(3)], axis=1)

        def vector(i):
            heads, tails = [], []
            for s in held:
                v = slots[s, X_ROWS + S_ROWS :, :].astype(jnp.float32)
                heads.append(v[3 * i : 3 * i + 1] + v[3 * i + 1 : 3 * i + 2] + v[3 * i + 2 : 3 * i + 3])
                j = 3 * i + 3
                tails.append(v[j : j + 1] + v[j + 1 : j + 2] + v[j + 2 : j + 3])
            heads.append(jnp.where(low, tails[0], tails[1]))
            heads.append(jnp.where(low, tails[2], tails[3]))
            return jnp.concatenate(heads, axis=1)

        return xs, ss, vector(0), vector(2)

    def contract(left, right):
        return lax.dot_general(
            left, right, (((1,), (1,)), ((), ())), preferred_element_type=jnp.float32
        )

    def tile_terms(g, loaded, i):
        xs, ss, sb, sc = loaded
        points = tile_points(i)
        base = jnp.concatenate([ta[i]] * 6, axis=1)
        kern = jnp.exp2(contract(points, xs) * LOG2E + (base + sb))
        weight = kern * (contract(points, ss) + sc)
        total = weight[:, :LANES]
        for q in range(1, 6):
            total = total + weight[:, q * LANES : (q + 1) * LANES]
        pair = jnp.concatenate([kern.astype(jnp.bfloat16), weight.astype(jnp.bfloat16)], axis=1)
        mixed = jnp.dot(
            pair, jnp.concatenate([ss, xs], axis=0), preferred_element_type=jnp.float32
        )
        if g > 0:
            mixed, total = mixed + acc[i], total + tot[i]
        return mixed, total

    def compute(g, tiles):
        loaded = sources(g)
        for i in tiles:
            mixed, total = tile_terms(g, loaded, i)
            acc[i] = mixed
            tot[i] = total

    pl.semaphore_wait(barrier, len(near))
    copies[1, 0, None].start()
    copies[3, 0, None].start()
    x_copies[0, 1].start()
    for t in (2, 1, 3):
        x_copies[t, 0].start()
        x_copies[t, 1].start()
    copies[0, 1, None].start()
    copies[0, 3, None].start()

    copies[3, 0, None].wait_recv()
    copies[2, 0, 0].start()
    copies[1, 0, None].wait_recv()
    copies[2, 0, 1].start()
    for f in (1, 3):
        copies[f, 1, None].start()
        copies[f, 3, None].start()

    def relay(f):
        copies[f, 3, None].wait_recv()
        copies[f, 2, 0].start()
        copies[f, 1, None].wait_recv()
        copies[f, 2, 1].start()

    def settle(f):
        copies[f, 2, 0].wait_recv()
        copies[f, 2, 1].wait_recv()

    x_copies[0, 1].wait_recv()
    target_base(0)
    for i, t in ((1, 1), (2, 3)):
        x_copies[t, 0].wait_recv()
        x_copies[t, 1].wait_recv()
        target_base(i)
    settle_first = (copies[2, 0, 0], copies[2, 0, 1])
    for copy in settle_first:
        copy.wait_recv()
    copies[2, 1, None].start()
    copies[2, 3, None].start()

    compute(0, (0, 1))
    relay(0)
    x_copies[2, 0].wait_recv()
    x_copies[2, 1].wait_recv()
    target_base(3)
    compute(0, (2, 3))
    relay(1)
    settle(0)
    compute(1, (0, 1))
    relay(3)
    compute(1, (2, 3))
    settle(1)
    compute(2, (0, 1))
    relay(2)
    compute(2, (2, 3))
    settle(3)
    settle(2)

    loaded = sources(3)
    for i in (3, 1, 2, 0):
        mixed, total = tile_terms(3, loaded, i)
        total = jnp.sum(total, axis=1, keepdims=True)
        mixed = mixed - tile_points(i).astype(jnp.float32) * total
        for k in range(2):
            n = 2 * i + k
            rows = slice(k * ROWS, (k + 1) * ROWS)
            line = jnp.broadcast_to(total[rows], (ROWS, LANES))
            line = jnp.concatenate([line, line[LANES:]], axis=0).T
            ptot[n] = line[0:1]
            if n == 0:
                acc[0, :ROWS, :] = mixed[rows]
                continue
            for p in range(2):
                part[n, p * ROWS : (p + 1) * ROWS, :] = mixed[
                    rows, p * LANES : (p + 1) * LANES
                ].astype(jnp.bfloat16)
            t = (RING - OFFSETS[i]) % RING
            r_copies[t, k].start()
            p_copies[t, k].start()

    image = acc[0, :ROWS, :]
    totals = ptot[0]
    for t in (0, 1, 3, 2):
        for k in range(2):
            if (t, k) == (0, 0):
                continue
            n = target_slot(t, k)
            r_copies[t, k].wait_recv()
            p_copies[t, k].wait_recv()
            image = image + jnp.concatenate([rsb[n, :ROWS, :], rsb[n, ROWS:, :]], axis=1).astype(jnp.float32)
            totals = totals + rst[n]
    dg, rg = dg_ref[...], rg_ref[...]
    dv, rv = dv_ref[...], rv_ref[...]
    image = jnp.sqrt(scale_ref[...]) * image + NUGGET * dg
    image_vals = totals[:, :ROWS] + NUGGET * dv

    def inner(vals, grads):
        first_part = jnp.sum(jnp.sum(grads, axis=0, keepdims=True), axis=1, keepdims=True)
        return first_part + jnp.sum(vals, axis=1, keepdims=True)

    sums = (
        inner(rv * rv, rg * rg),
        inner(dv * image_vals, dg * image),
        inner(rv * image_vals, rg * image),
        inner(image_vals * image_vals, image * image),
    )
    lane_row = lax.broadcasted_iota(jnp.int32, (1, LANES), 1)
    packed = jnp.zeros((1, LANES), jnp.float32)
    for i, value in enumerate(sums):
        packed = jnp.where(lane_row == i, value, packed)
    mine[...] = packed

    me = row * 8 + col

    def spread(i, carry):
        peer = (me + i) % COUNT
        pltpu.make_async_remote_copy(
            src_ref=mine,
            dst_ref=arb.at[me],
            send_sem=a_send,
            recv_sem=a_recv,
            device_id=(peer // 8, peer % 8),
            device_id_type=MESH,
        ).start()
        return carry

    lax.fori_loop(1, COUNT, spread, 0)
    arb[me] = packed
    others = arb.at[pl.ds(0, COUNT - 1)]
    pltpu.make_async_copy(others, others, a_recv).wait()

    every = jnp.sum(arb[...], axis=0)

    def pick(i):
        return jnp.sum(jnp.where(lane_row == i, every, 0.0), axis=1, keepdims=True)

    norm_now, curvature, cross, image_norm = (pick(i) for i in range(4))
    step = norm_now / curvature
    norm_next = norm_now - 2.0 * (step * cross) + step * (step * image_norm)
    ratio = norm_next / norm_now
    next_vals = rv - step * image_vals
    next_grads = rg - step * image
    nsv_ref[...] = sv_ref[...] + step * dv
    nsg_ref[...] = sg_ref[...] + step * dg
    nrv_ref[...] = next_vals
    nrg_ref[...] = next_grads
    ndv_ref[...] = next_vals + ratio * dv
    ndg_ref[...] = next_grads + ratio * dg

    for copy in copies.values():
        copy.wait_send()
    for group in (x_copies, r_copies, p_copies):
        for copy in group.values():
            copy.wait_send()
    pltpu.make_async_copy(others, others, a_send).wait()


def body(points, lengthscale, sv, sg, rv, rg, dv, dg):
    vmem = pl.BlockSpec(memory_space=pltpu.VMEM)
    line = jax.ShapeDtypeStruct((1, ROWS), jnp.float32)
    block = jax.ShapeDtypeStruct((ROWS, DIM), jnp.float32)
    dma = pltpu.SemaphoreType.DMA
    outs = pl.pallas_call(
        kernel,
        out_shape=(line, block) * 3,
        in_specs=[vmem] * 8,
        out_specs=(vmem,) * 6,
        scratch_shapes=[
            pltpu.VMEM((16, BLOCK, LANES), jnp.bfloat16),
            pltpu.VMEM((8, X_ROWS, LANES), jnp.bfloat16),
            pltpu.VMEM((4, 2 * ROWS, LANES), jnp.float32),
            pltpu.VMEM((4, 2 * ROWS, DIM), jnp.float32),
            pltpu.VMEM((4, 2 * ROWS, LANES), jnp.float32),
            pltpu.VMEM((8, X_ROWS, LANES), jnp.bfloat16),
            pltpu.VMEM((8, 1, 2 * LANES), jnp.float32),
            pltpu.VMEM((8, X_ROWS, LANES), jnp.bfloat16),
            pltpu.VMEM((8, 1, 2 * LANES), jnp.float32),
            pltpu.VMEM((V_ROWS, LANES), jnp.float32),
            pltpu.VMEM((1, LANES), jnp.float32),
            pltpu.VMEM((COUNT, 1, LANES), jnp.float32),
            dma((20,)),
            dma((20,)),
            dma((8,)),
            dma((8,)),
            dma((8,)),
            dma((8,)),
            dma((8,)),
            dma((8,)),
            dma,
            dma,
        ],
        compiler_params=pltpu.CompilerParams(
            collective_id=0, has_side_effects=True, vmem_limit_bytes=48 << 20
        ),
        cost_estimate=pl.CostEstimate(
            flops=9_700_000_000, bytes_accessed=2_000_000, transcendentals=4_800_000
        ),
    )(
        points,
        lengthscale.reshape(1, DIM),
        sv.reshape(1, ROWS),
        sg,
        rv.reshape(1, ROWS),
        rg,
        dv.reshape(1, ROWS),
        dg,
    )
    nsv, nsg, nrv, nrg, ndv, ndg = outs
    return (nsv.reshape(ROWS), nsg, nrv.reshape(ROWS), nrg, ndv.reshape(ROWS), ndg)


def solution(mesh):
    lines, blocks = P(("row", "col")), P(("row", "col"), None)
    return jax.shard_map(
        body,
        mesh=mesh,
        in_specs=(blocks, P(), lines, blocks, lines, blocks, lines, blocks),
        out_specs=(lines, blocks) * 3,
        check_vma=False,
    )
```

```python
import functools
import math

import jax
import jax.numpy as jnp
from jax import lax
from jax.experimental import pallas as pl
from jax.experimental.pallas import tpu as pltpu
from jax.sharding import PartitionSpec as P

MESH = pl.DeviceIdType.MESH
LOG2E = math.log2(math.e)
NUGGET = 4.0
RING = 4
ROWS = 192
DIM = 256
LANES = 128
TAIL = ROWS - LANES
X_ROWS = 2 * ROWS
PLANES = (0, ROWS, 2 * ROWS, 3 * ROWS + 16)
VECTORS = slice(3 * ROWS, 3 * ROWS + 16)
BLOCK = 4 * ROWS + 16
SPLIT = PLANES[3]
CUT = 288
OFFSETS = (0, 1, 3, 2)
COUNT = 128
GRANT = 62 << 20
ORDER = (
    ((0, 0), (1, 0), (3, 0), (0, 1))
    + ((0, 3), (2, 0), (0, 2), (1, 1))
    + ((1, 3), (3, 1), (3, 3), (2, 1))
    + ((2, 3), (1, 2), (3, 2), (2, 2))
)


def slot_of(f, s):
    return ORDER.index((f, s))


def target_slot(t, k):
    return 2 * OFFSETS.index(t % RING) + k


def kernel(
    points_hbm,
    scale_hbm,
    rv_hbm,
    rg_hbm,
    dv_hbm,
    dg_hbm,
    vals_hbm,
    image_hbm,
    steps_hbm,
    vals_ref,
    image_ref,
    points_ref,
    scale_ref,
    rv_ref,
    rg_ref,
    dv_ref,
    dg_ref,
    slots,
    tx,
    ta,
    acc,
    tot,
    part,
    ptot,
    rsb,
    rst,
    vecs,
    mine,
    arb,
    g_send,
    g_recv,
    x_send,
    x_recv,
    r_send,
    r_recv,
    p_send,
    p_recv,
    a_send,
    a_recv,
    loads,
):
    row, col = lax.axis_index("row"), lax.axis_index("col")
    z, y = row // RING, row % RING
    x, c = col // 2, col % 2
    o = 1 - c

    def first(d):
        return (z * RING + (y + d) % RING, col)

    def second(d, core):
        return (((z + o * d) % RING) * RING + y, ((x + c * d) % RING) * 2 + core)

    def third(d, core):
        return (((z + c * d) % RING) * RING + y, ((x + o * d) % RING) * 2 + core)

    barrier = pltpu.get_barrier_semaphore()
    near = [first(1), first(3), second(1, c), second(3, c)]
    near += [third(t, c) for t in (1, 2, 3)] + [third(t, o) for t in range(RING)]
    near += [second(t, o) for t in (1, 2, 3)]
    for peer in near:
        pl.semaphore_signal(barrier, inc=1, device_id=peer, device_id_type=MESH)

    pairs = (
        (points_hbm, points_ref),
        (scale_hbm, scale_ref),
        (dg_hbm, dg_ref),
        (dv_hbm, dv_ref),
        (rg_hbm, rg_ref),
        (rv_hbm, rv_ref),
    )
    arrivals = [pltpu.make_async_copy(a, b, loads.at[i]) for i, (a, b) in enumerate(pairs)]
    for arrival in arrivals:
        arrival.start()
    for arrival in arrivals[:4]:
        arrival.wait()

    root = jnp.sqrt(scale_ref[...])
    scaled = (points_ref[...].astype(jnp.float32) * root).astype(jnp.bfloat16)
    slope = (dg_ref[...] * root).astype(jnp.bfloat16)
    for p in range(2):
        lanes = slice(p * LANES, (p + 1) * LANES)
        slots[0, p * ROWS : (p + 1) * ROWS, :] = scaled[:, lanes]
        slots[0, PLANES[2 + p] : PLANES[2 + p] + ROWS, :] = slope[:, lanes]
        tx[0, p * ROWS : (p + 1) * ROWS, :] = scaled[:, lanes]
    wide = scaled.astype(jnp.float32)
    square = jnp.sum(wide * wide, axis=1, keepdims=True)
    shift = jnp.sum(wide * slope.astype(jnp.float32), axis=1, keepdims=True)
    lane = lax.broadcasted_iota(jnp.int32, (ROWS, LANES), 1)
    both = jnp.where(lane == 0, square, jnp.where(lane == 1, shift, 0.0))
    both = jnp.concatenate([both, both[LANES:]], axis=0)
    across = both.T
    level = dv_ref[...].astype(jnp.bfloat16).astype(jnp.float32)
    base = across[0:1] * (-0.5 * LOG2E)
    terms = (
        base[:, :LANES],
        base[:, LANES:],
        level[:, :LANES] - across[1:2, :LANES],
        jnp.concatenate([level[:, LANES:], level[:, LANES:]], axis=1) - across[1:2, LANES:],
    )
    vecs[...] = jnp.zeros_like(vecs)
    for i, term in enumerate(terms):
        for j in range(3):
            piece = term.astype(jnp.bfloat16).astype(jnp.float32)
            vecs[3 * i + j : 3 * i + j + 1, :] = piece
            term = term - piece
    slots[0, VECTORS, :] = vecs[...].astype(jnp.bfloat16)

    upper, lower = {}, {}

    def describe(group, key, slot, source, top, stop, peer):
        n = len(upper) + len(lower)
        group[key] = pltpu.make_async_remote_copy(
            src_ref=slots.at[source, pl.ds(top, stop - top)],
            dst_ref=slots.at[slot, pl.ds(top, stop - top)],
            send_sem=g_send.at[n],
            recv_sem=g_recv.at[n],
            device_id=peer,
            device_id_type=MESH,
        )

    def whole(f, s, source, peer):
        describe(upper, (f, s), slot_of(f, s), slot_of(*source), 0, SPLIT, peer)

    def halves(f, s, behind, ahead, forward, back):
        describe(upper, (f, s, 0), slot_of(f, s), slot_of(*behind), 0, CUT, forward)
        describe(upper, (f, s, 1), slot_of(f, s), slot_of(*ahead), CUT, SPLIT, back)

    whole(1, 0, (0, 0), first(3))
    whole(3, 0, (0, 0), first(1))
    halves(2, 0, (3, 0), (1, 0), first(1), first(3))
    for f in OFFSETS:
        whole(f, 1, (f, 0), second(3, c))
        whole(f, 3, (f, 0), second(1, c))
        halves(f, 2, (f, 3), (f, 1), second(1, c), second(3, c))

    def other(f, s, source, peer):
        describe(lower, (f, s), slot_of(f, s), source, SPLIT, BLOCK, peer)

    def across_core(behind, ahead):
        return slot_of(*behind) * o + slot_of(*ahead) * c

    away = 1 + 2 * c
    other(0, 1, slot_of(0, 0), second(3, c))
    other(0, 3, slot_of(0, 0), second(1, c))
    other(0, 2, across_core((0, 3), (0, 1)), second(away, c))
    for s in OFFSETS:
        other(1, s, slot_of(0, s), first(3))
        other(3, s, slot_of(0, s), first(1))
        other(2, s, across_core((3, s), (1, s)), first(away))

    x_copies, r_copies, p_copies = {}, {}, {}
    for t in OFFSETS:
        for k in range(2):
            if (t, k) == (0, 0):
                continue
            n = target_slot(t, k)
            back = (RING - t) % RING
            x_copies[t, k] = pltpu.make_async_remote_copy(
                src_ref=slots.at[0, pl.ds(0, X_ROWS)],
                dst_ref=tx.at[n],
                send_sem=x_send.at[n],
                recv_sem=x_recv.at[n],
                device_id=second(back, o) if k else third(back, c),
                device_id_type=MESH,
            )
            owner = third(back, o) if k else third(back, c)
            r_copies[t, k] = pltpu.make_async_remote_copy(
                src_ref=part.at[target_slot(back, k)],
                dst_ref=rsb.at[n],
                send_sem=r_send.at[n],
                recv_sem=r_recv.at[n],
                device_id=owner,
                device_id_type=MESH,
            )
            p_copies[t, k] = pltpu.make_async_remote_copy(
                src_ref=ptot.at[target_slot(back, k)],
                dst_ref=rst.at[n],
                send_sem=p_send.at[n],
                recv_sem=p_recv.at[n],
                device_id=owner,
                device_id_type=MESH,
            )

    def tile_points(i):
        planes = []
        for p in range(2):
            rows = slice(p * ROWS, (p + 1) * ROWS)
            planes.append(jnp.concatenate([tx[2 * i, rows, :], tx[2 * i + 1, rows, :]], axis=0))
        return jnp.concatenate(planes, axis=1)

    def target_base(i):
        value = tile_points(i).astype(jnp.float32)
        total = jnp.sum(value * value, axis=1, keepdims=True) * (-0.5 * LOG2E)
        ta[i] = jnp.broadcast_to(total, (2 * ROWS, LANES))

    low = lax.broadcasted_iota(jnp.int32, (1, LANES), 1) < TAIL

    def sources(heads, tails):
        def plane(p):
            top = PLANES[p]
            pieces = [slots[s, top : top + LANES, :] for s in heads]
            pieces += [slots[s, top + LANES : top + ROWS, :] for s in tails]
            return jnp.concatenate(pieces, axis=0)

        xs = jnp.concatenate([plane(0), plane(1)], axis=1)
        ss = jnp.concatenate([plane(2), plane(3)], axis=1)

        def vector(i):
            def read(s, j):
                v = slots[s, VECTORS, :].astype(jnp.float32)
                return v[j : j + 1] + v[j + 1 : j + 2] + v[j + 2 : j + 3]

            pieces = [read(s, 3 * i) for s in heads]
            ends = [read(s, 3 * i + 3) for s in tails]
            pieces += [jnp.where(low, u, v) for u, v in zip(ends[::2], ends[1::2])]
            return jnp.concatenate(pieces, axis=1)

        return xs, ss, vector(0), vector(2)

    def contract(left, right):
        return lax.dot_general(
            left, right, (((1,), (1,)), ((), ())), preferred_element_type=jnp.float32
        )

    def tile_terms(loaded, i, fresh=False):
        xs, ss, sb, sc = loaded
        points = tile_points(i)
        wide = xs.shape[0] // LANES
        base = jnp.concatenate([ta[i]] * wide, axis=1)
        kern = jnp.exp2(contract(points, xs) * LOG2E + (base + sb))
        weight = kern * (contract(points, ss) + sc)
        total = weight[:, :LANES]
        for q in range(1, wide):
            total = total + weight[:, q * LANES : (q + 1) * LANES]
        pair = jnp.concatenate([kern.astype(jnp.bfloat16), weight.astype(jnp.bfloat16)], axis=1)
        mixed = jnp.dot(
            pair, jnp.concatenate([ss, xs], axis=0), preferred_element_type=jnp.float32
        )
        if not fresh:
            mixed, total = mixed + acc[i], total + tot[i]
        return mixed, total

    def compute(g, tiles):
        held = range(4 * g, 4 * g + 4)
        loaded = sources(held, held)
        for i in tiles:
            mixed, total = tile_terms(loaded, i, fresh=g == 0)
            acc[i] = mixed
            tot[i] = total

    def start(*some):
        for copy in some:
            copy.start()

    def landed(*some):
        for copy in some:
            copy.wait_recv()

    pl.semaphore_wait(barrier, len(near))
    start(upper[1, 0], upper[3, 0], lower[0, 1], lower[0, 3])
    start(x_copies[0, 1])
    for t in (2, 1, 3):
        start(x_copies[t, 0], x_copies[t, 1])
    start(upper[0, 1], upper[0, 3], lower[1, 0], lower[3, 0])

    landed(lower[0, 1], lower[0, 3])
    start(lower[0, 2])
    start(*(lower[f, s] for s in (1, 3) for f in (1, 3)))
    landed(upper[3, 0], upper[1, 0])
    start(upper[2, 0, 0], upper[2, 0, 1])
    start(*(upper[f, s] for f in (1, 3) for s in (1, 3)))

    landed(x_copies[0, 1])
    target_base(0)
    for i, t in ((1, 1), (2, 3)):
        landed(x_copies[t, 0], x_copies[t, 1])
        target_base(i)
    landed(upper[0, 3], upper[0, 1])
    start(upper[0, 2, 0], upper[0, 2, 1])
    landed(lower[1, 0], lower[3, 0])
    start(lower[2, 0])
    compute(0, (0, 1))

    landed(x_copies[2, 0], x_copies[2, 1])
    target_base(3)
    landed(lower[0, 2])
    start(lower[1, 2], lower[3, 2])
    landed(upper[2, 0, 0], upper[2, 0, 1])
    start(upper[2, 1], upper[2, 3])
    compute(0, (2, 3))

    landed(lower[1, 1], lower[3, 1], lower[1, 3], lower[3, 3])
    start(lower[2, 1], lower[2, 3])
    landed(upper[1, 1], upper[1, 3])
    start(upper[1, 2, 0], upper[1, 2, 1])
    landed(upper[3, 1], upper[3, 3])
    start(upper[3, 2, 0], upper[3, 2, 1])
    landed(upper[0, 2, 0], upper[0, 2, 1], lower[2, 0])
    compute(1, (0, 1))
    landed(lower[1, 2], lower[3, 2])
    start(lower[2, 2])
    compute(1, (2, 3))
    landed(upper[2, 1], upper[2, 3])
    start(upper[2, 2, 0], upper[2, 2, 1])
    landed(lower[2, 1])
    compute(2, (0, 1, 2, 3))
    landed(lower[2, 3], upper[1, 2, 0], upper[1, 2, 1], upper[3, 2, 0], upper[3, 2, 1])
    loaded = sources((12, 13, 14), (12, 13))
    for i in range(4):
        acc[i], tot[i] = tile_terms(loaded, i)
    landed(lower[2, 2], upper[2, 2, 0], upper[2, 2, 1])

    loaded = sources((15,), (14, 15))
    for i in (3, 1, 2, 0):
        mixed, total = tile_terms(loaded, i)
        total = jnp.sum(total, axis=1, keepdims=True)
        mixed = mixed - tile_points(i).astype(jnp.float32) * total
        for k in range(2):
            n = 2 * i + k
            rows = slice(k * ROWS, (k + 1) * ROWS)
            line = jnp.broadcast_to(total[rows], (ROWS, LANES))
            line = jnp.concatenate([line, line[LANES:]], axis=0).T
            ptot[n] = line[0:1]
            if n == 0:
                acc[0, :ROWS, :] = mixed[rows]
                continue
            for p in range(2):
                part[n, p * ROWS : (p + 1) * ROWS, :] = mixed[
                    rows, p * LANES : (p + 1) * LANES
                ].astype(jnp.bfloat16)
            t = (RING - OFFSETS[i]) % RING
            r_copies[t, k].start()
            p_copies[t, k].start()

    image = acc[0, :ROWS, :]
    totals = ptot[0]
    for t in (0, 1, 3, 2):
        for k in range(2):
            if (t, k) == (0, 0):
                continue
            n = target_slot(t, k)
            r_copies[t, k].wait_recv()
            p_copies[t, k].wait_recv()
            image = image + jnp.concatenate([rsb[n, :ROWS, :], rsb[n, ROWS:, :]], axis=1).astype(jnp.float32)
            totals = totals + rst[n]
    for arrival in arrivals[4:]:
        arrival.wait()
    dg, rg = dg_ref[...], rg_ref[...]
    dv, rv = dv_ref[...], rv_ref[...]
    image = jnp.sqrt(scale_ref[...]) * image + NUGGET * dg
    image_vals = totals[:, :ROWS] + NUGGET * dv

    vals_ref[...] = image_vals
    image_ref[...] = image
    stores = [
        pltpu.make_async_copy(vals_ref, vals_hbm, loads.at[1]),
        pltpu.make_async_copy(image_ref, image_hbm, loads.at[2]),
    ]
    for store in stores:
        store.start()

    def inner(vals, grads):
        first_part = jnp.sum(jnp.sum(grads, axis=0, keepdims=True), axis=1, keepdims=True)
        return first_part + jnp.sum(vals, axis=1, keepdims=True)

    sums = (
        inner(rv * rv, rg * rg),
        inner(dv * image_vals, dg * image),
        inner(rv * image_vals, rg * image),
        inner(image_vals * image_vals, image * image),
    )
    lane_row = lax.broadcasted_iota(jnp.int32, (1, LANES), 1)
    packed = jnp.zeros((1, LANES), jnp.float32)
    for i, value in enumerate(sums):
        packed = jnp.where(lane_row == i, value, packed)
    mine[...] = packed

    me = row * 8 + col

    def spread(i, carry):
        peer = (me + i) % COUNT
        pltpu.make_async_remote_copy(
            src_ref=mine,
            dst_ref=arb.at[me],
            send_sem=a_send,
            recv_sem=a_recv,
            device_id=(peer // 8, peer % 8),
            device_id_type=MESH,
        ).start()
        return carry

    lax.fori_loop(1, COUNT, spread, 0)
    arb[me] = packed
    others = arb.at[pl.ds(0, COUNT - 1)]
    pltpu.make_async_copy(others, others, a_recv).wait()

    every = jnp.sum(arb[...], axis=0)

    def pick(i):
        return jnp.sum(jnp.where(lane_row == i, every, 0.0), axis=1, keepdims=True)

    norm_now, curvature, cross, image_norm = (pick(i) for i in range(4))
    step = norm_now / curvature
    norm_next = norm_now - 2.0 * (step * cross) + step * (step * image_norm)
    ratio = norm_next / norm_now
    pltpu.make_async_copy(others, others, a_send).wait()
    mine[...] = jnp.where(lane_row == 0, step, ratio)
    last = pltpu.make_async_copy(mine, steps_hbm, loads.at[0])
    last.start()

    for group in (upper, lower, x_copies, r_copies, p_copies):
        for copy in group.values():
            copy.wait_send()
    for store in stores:
        store.wait()
    last.wait()


def update(*refs):
    sources, results, held = refs[:9], refs[9:15], refs[15:29]
    steps, arrived, left = refs[29:]
    landing = held[:8] + (steps,)
    loads = [pltpu.make_async_copy(a, b, arrived.at[i]) for i, (a, b) in enumerate(zip(sources, landing))]
    for load in loads:
        load.start()
    for load in loads:
        load.wait()
    sv, sg, rv, rg, dv, dg, iv, ig = (ref[...] for ref in landing[:8])
    step, ratio = steps[:, 0:1], steps[:, 1:2]
    nrv, nrg = rv - step * iv, rg - step * ig
    values = (sv + step * dv, sg + step * dg, nrv, nrg, nrv + ratio * dv, nrg + ratio * dg)
    stores = []
    for i, value in enumerate(values):
        held[8 + i][...] = value
        stores.append(pltpu.make_async_copy(held[8 + i], results[i], left.at[i]))
        stores[i].start()
    for store in stores:
        store.wait()


def body(points, lengthscale, sv, sg, rv, rg, dv, dg):
    hbm = pl.BlockSpec(memory_space=pltpu.HBM)
    line = jax.ShapeDtypeStruct((1, ROWS), jnp.float32)
    block = jax.ShapeDtypeStruct((ROWS, DIM), jnp.float32)
    dma = pltpu.SemaphoreType.DMA
    image_vals, image_grads, steps = pl.pallas_call(
        kernel,
        out_shape=(line, block, jax.ShapeDtypeStruct((1, LANES), jnp.float32)),
        in_specs=[hbm] * 6,
        out_specs=(hbm,) * 3,
        scratch_shapes=[
            pltpu.VMEM((1, ROWS), jnp.float32),
            pltpu.VMEM((ROWS, DIM), jnp.float32),
            pltpu.VMEM((ROWS, DIM), jnp.bfloat16),
            pltpu.VMEM((1, DIM), jnp.float32),
            pltpu.VMEM((1, ROWS), jnp.float32),
            pltpu.VMEM((ROWS, DIM), jnp.float32),
            pltpu.VMEM((1, ROWS), jnp.float32),
            pltpu.VMEM((ROWS, DIM), jnp.float32),
            pltpu.VMEM((16, BLOCK, LANES), jnp.bfloat16),
            pltpu.VMEM((8, X_ROWS, LANES), jnp.bfloat16),
            pltpu.VMEM((4, 2 * ROWS, LANES), jnp.float32),
            pltpu.VMEM((4, 2 * ROWS, DIM), jnp.float32),
            pltpu.VMEM((4, 2 * ROWS, LANES), jnp.float32),
            pltpu.VMEM((8, X_ROWS, LANES), jnp.bfloat16),
            pltpu.VMEM((8, 1, 2 * LANES), jnp.float32),
            pltpu.VMEM((8, X_ROWS, LANES), jnp.bfloat16),
            pltpu.VMEM((8, 1, 2 * LANES), jnp.float32),
            pltpu.VMEM((16, LANES), jnp.float32),
            pltpu.VMEM((1, LANES), jnp.float32),
            pltpu.VMEM((COUNT, 1, LANES), jnp.float32),
            dma((35,)),
            dma((35,)),
            dma((8,)),
            dma((8,)),
            dma((8,)),
            dma((8,)),
            dma((8,)),
            dma((8,)),
            dma,
            dma,
            dma((6,)),
        ],
        compiler_params=pltpu.CompilerParams(
            collective_id=0, has_side_effects=True, vmem_limit_bytes=GRANT
        ),
        cost_estimate=pl.CostEstimate(
            flops=9_700_000_000, bytes_accessed=2_000_000, transcendentals=4_800_000
        ),
    )(
        points,
        lengthscale.reshape(1, DIM),
        rv.reshape(1, ROWS),
        rg,
        dv.reshape(1, ROWS),
        dg,
    )
    nsv, nsg, nrv, nrg, ndv, ndg = pl.pallas_call(
        update,
        out_shape=(line, block) * 3,
        in_specs=[hbm] * 9,
        out_specs=(hbm,) * 6,
        scratch_shapes=[pltpu.VMEM((1, ROWS), jnp.float32), pltpu.VMEM((ROWS, DIM), jnp.float32)] * 7
        + [pltpu.VMEM((1, LANES), jnp.float32), dma((9,)), dma((6,))],
        compiler_params=pltpu.CompilerParams(vmem_limit_bytes=GRANT),
    )(
        sv.reshape(1, ROWS),
        sg,
        rv.reshape(1, ROWS),
        rg,
        dv.reshape(1, ROWS),
        dg,
        image_vals,
        image_grads,
        steps,
    )
    return (nsv.reshape(ROWS), nsg, nrv.reshape(ROWS), nrg, ndv.reshape(ROWS), ndg)


def solution(mesh):
    lines, blocks = P(("row", "col")), P(("row", "col"), None)
    return jax.shard_map(
        body,
        mesh=mesh,
        in_specs=(blocks, P(), lines, blocks, lines, blocks, lines, blocks),
        out_specs=(lines, blocks) * 3,
        check_vma=False,
    )
```

```python
import functools
import math

import jax
import jax.numpy as jnp
from jax import lax
from jax.experimental import pallas as pl
from jax.experimental.pallas import tpu as pltpu
from jax.sharding import PartitionSpec as P

MESH = pl.DeviceIdType.MESH
LOG2E = math.log2(math.e)
NUGGET = 4.0
RING = 4
ROWS = 192
DIM = 256
LANES = 128
TAIL = ROWS - LANES
X_ROWS = 2 * ROWS
PLANES = (0, ROWS, 2 * ROWS, 3 * ROWS + 16)
VECTORS = slice(3 * ROWS, 3 * ROWS + 16)
BLOCK = 4 * ROWS + 16
SPLIT = PLANES[3]
CUT = 288
OFFSETS = (0, 1, 3, 2)
COUNT = 128
GRANT = 62 << 20
ORDER = (
    ((0, 0), (1, 0), (3, 0))
    + ((0, 1), (0, 3), (2, 0))
    + ((1, 1), (1, 3), (3, 1), (3, 3))
    + ((0, 2), (2, 1), (2, 3))
    + ((1, 2), (3, 2), (2, 2))
)
GROUPS = (
    ((0, 1, 2), (0, 1)),
    ((3, 4, 5), (2, 3, 4, 5)),
    ((6, 7, 8, 9), (6, 7, 8, 9)),
    ((10, 11, 12), (10, 11)),
    ((13, 14, 15), (12, 13, 14, 15)),
)


def slot_of(f, s):
    return ORDER.index((f, s))


def target_slot(t, k):
    return 2 * OFFSETS.index(t % RING) + k


def kernel(
    points_hbm,
    scale_hbm,
    rv_hbm,
    rg_hbm,
    dv_hbm,
    dg_hbm,
    vals_hbm,
    image_hbm,
    steps_hbm,
    vals_ref,
    image_ref,
    points_ref,
    scale_ref,
    rv_ref,
    rg_ref,
    dv_ref,
    dg_ref,
    slots,
    tx,
    ta,
    acc,
    tot,
    part,
    ptot,
    rsb,
    rst,
    vecs,
    mine,
    arb,
    g_send,
    g_recv,
    x_send,
    x_recv,
    r_send,
    r_recv,
    p_send,
    p_recv,
    a_send,
    a_recv,
    loads,
):
    row, col = lax.axis_index("row"), lax.axis_index("col")
    z, y = row // RING, row % RING
    x, c = col // 2, col % 2
    o = 1 - c

    def first(d):
        return (z * RING + (y + d) % RING, col)

    def second(d, core):
        return (((z + o * d) % RING) * RING + y, ((x + c * d) % RING) * 2 + core)

    def third(d, core):
        return (((z + c * d) % RING) * RING + y, ((x + o * d) % RING) * 2 + core)

    barrier = pltpu.get_barrier_semaphore()
    near = [first(1), first(3), second(1, c), second(3, c)]
    near += [third(t, c) for t in (1, 2, 3)] + [third(t, o) for t in range(RING)]
    near += [second(t, o) for t in (1, 2, 3)]
    for peer in near:
        pl.semaphore_signal(barrier, inc=1, device_id=peer, device_id_type=MESH)

    pairs = (
        (points_hbm, points_ref),
        (scale_hbm, scale_ref),
        (dg_hbm, dg_ref),
        (dv_hbm, dv_ref),
        (rg_hbm, rg_ref),
        (rv_hbm, rv_ref),
    )
    arrivals = [pltpu.make_async_copy(a, b, loads.at[i]) for i, (a, b) in enumerate(pairs)]
    for arrival in arrivals:
        arrival.start()
    for arrival in arrivals[:4]:
        arrival.wait()

    root = jnp.sqrt(scale_ref[...])
    scaled = (points_ref[...].astype(jnp.float32) * root).astype(jnp.bfloat16)
    slope = (dg_ref[...] * root).astype(jnp.bfloat16)
    for p in range(2):
        lanes = slice(p * LANES, (p + 1) * LANES)
        slots[0, p * ROWS : (p + 1) * ROWS, :] = scaled[:, lanes]
        slots[0, PLANES[2 + p] : PLANES[2 + p] + ROWS, :] = slope[:, lanes]
        tx[0, p * ROWS : (p + 1) * ROWS, :] = scaled[:, lanes]
    wide = scaled.astype(jnp.float32)
    square = jnp.sum(wide * wide, axis=1, keepdims=True)
    shift = jnp.sum(wide * slope.astype(jnp.float32), axis=1, keepdims=True)
    lane = lax.broadcasted_iota(jnp.int32, (ROWS, LANES), 1)
    both = jnp.where(lane == 0, square, jnp.where(lane == 1, shift, 0.0))
    both = jnp.concatenate([both, both[LANES:]], axis=0)
    across = both.T
    level = dv_ref[...].astype(jnp.bfloat16).astype(jnp.float32)
    base = across[0:1] * (-0.5 * LOG2E)
    terms = (
        base[:, :LANES],
        base[:, LANES:],
        level[:, :LANES] - across[1:2, :LANES],
        jnp.concatenate([level[:, LANES:], level[:, LANES:]], axis=1) - across[1:2, LANES:],
    )
    vecs[...] = jnp.zeros_like(vecs)
    for i, term in enumerate(terms):
        for j in range(3):
            piece = term.astype(jnp.bfloat16).astype(jnp.float32)
            vecs[3 * i + j : 3 * i + j + 1, :] = piece
            term = term - piece
    slots[0, VECTORS, :] = vecs[...].astype(jnp.bfloat16)

    upper, lower = {}, {}

    def describe(group, key, slot, source, top, stop, peer):
        n = len(upper) + len(lower)
        group[key] = pltpu.make_async_remote_copy(
            src_ref=slots.at[source, pl.ds(top, stop - top)],
            dst_ref=slots.at[slot, pl.ds(top, stop - top)],
            send_sem=g_send.at[n],
            recv_sem=g_recv.at[n],
            device_id=peer,
            device_id_type=MESH,
        )

    def pieces(f, s, source, peer):
        describe(upper, (f, s, 0), slot_of(f, s), slot_of(*source), 0, CUT, peer)
        describe(upper, (f, s, 1), slot_of(f, s), slot_of(*source), CUT, SPLIT, peer)

    def whole(f, s, source, peer):
        describe(upper, (f, s), slot_of(f, s), slot_of(*source), 0, SPLIT, peer)

    def halves(f, s, behind, ahead, forward, back):
        describe(upper, (f, s, 0), slot_of(f, s), slot_of(*behind), 0, CUT, forward)
        describe(upper, (f, s, 1), slot_of(f, s), slot_of(*ahead), CUT, SPLIT, back)

    pieces(1, 0, (0, 0), first(3))
    pieces(3, 0, (0, 0), first(1))
    halves(2, 0, (3, 0), (1, 0), first(1), first(3))
    for f in OFFSETS:
        cast = pieces if f == 2 else whole
        cast(f, 1, (f, 0), second(3, c))
        cast(f, 3, (f, 0), second(1, c))
        halves(f, 2, (f, 3), (f, 1), second(1, c), second(3, c))

    def other(f, s, source, peer):
        describe(lower, (f, s), slot_of(f, s), source, SPLIT, BLOCK, peer)

    def across_core(behind, ahead):
        return slot_of(*behind) * o + slot_of(*ahead) * c

    away = 1 + 2 * c
    other(0, 1, slot_of(0, 0), second(3, c))
    other(0, 3, slot_of(0, 0), second(1, c))
    other(0, 2, across_core((0, 3), (0, 1)), second(away, c))
    for s in OFFSETS:
        other(1, s, slot_of(0, s), first(3))
        other(3, s, slot_of(0, s), first(1))
        other(2, s, across_core((3, s), (1, s)), first(away))

    x_copies, r_copies, p_copies = {}, {}, {}
    for t in OFFSETS:
        for k in range(2):
            if (t, k) == (0, 0):
                continue
            n = target_slot(t, k)
            back = (RING - t) % RING
            x_copies[t, k] = pltpu.make_async_remote_copy(
                src_ref=slots.at[0, pl.ds(0, X_ROWS)],
                dst_ref=tx.at[n],
                send_sem=x_send.at[n],
                recv_sem=x_recv.at[n],
                device_id=second(back, o) if k else third(back, c),
                device_id_type=MESH,
            )
            owner = third(back, o) if k else third(back, c)
            r_copies[t, k] = pltpu.make_async_remote_copy(
                src_ref=part.at[target_slot(back, k)],
                dst_ref=rsb.at[n],
                send_sem=r_send.at[n],
                recv_sem=r_recv.at[n],
                device_id=owner,
                device_id_type=MESH,
            )
            p_copies[t, k] = pltpu.make_async_remote_copy(
                src_ref=ptot.at[target_slot(back, k)],
                dst_ref=rst.at[n],
                send_sem=p_send.at[n],
                recv_sem=p_recv.at[n],
                device_id=owner,
                device_id_type=MESH,
            )

    def tile_points(i):
        planes = []
        for p in range(2):
            rows = slice(p * ROWS, (p + 1) * ROWS)
            planes.append(jnp.concatenate([tx[2 * i, rows, :], tx[2 * i + 1, rows, :]], axis=0))
        return jnp.concatenate(planes, axis=1)

    def target_base(i):
        value = tile_points(i).astype(jnp.float32)
        total = jnp.sum(value * value, axis=1, keepdims=True) * (-0.5 * LOG2E)
        ta[i] = jnp.broadcast_to(total, (2 * ROWS, LANES))

    low = lax.broadcasted_iota(jnp.int32, (1, LANES), 1) < TAIL

    def sources(heads, tails):
        def plane(p):
            top = PLANES[p]
            pieces = [slots[s, top : top + LANES, :] for s in heads]
            pieces += [slots[s, top + LANES : top + ROWS, :] for s in tails]
            return jnp.concatenate(pieces, axis=0)

        xs = jnp.concatenate([plane(0), plane(1)], axis=1)
        ss = jnp.concatenate([plane(2), plane(3)], axis=1)

        def vector(i):
            def read(s, j):
                v = slots[s, VECTORS, :].astype(jnp.float32)
                return v[j : j + 1] + v[j + 1 : j + 2] + v[j + 2 : j + 3]

            pieces = [read(s, 3 * i) for s in heads]
            ends = [read(s, 3 * i + 3) for s in tails]
            pieces += [jnp.where(low, u, v) for u, v in zip(ends[::2], ends[1::2])]
            return jnp.concatenate(pieces, axis=1)

        return xs, ss, vector(0), vector(2)

    def contract(left, right):
        return lax.dot_general(
            left, right, (((1,), (1,)), ((), ())), preferred_element_type=jnp.float32
        )

    def tile_terms(loaded, i, fresh=False):
        xs, ss, sb, sc = loaded
        points = tile_points(i)
        wide = xs.shape[0] // LANES
        base = jnp.concatenate([ta[i]] * wide, axis=1)
        kern = jnp.exp2(contract(points, xs) * LOG2E + (base + sb))
        weight = kern * (contract(points, ss) + sc)
        total = weight[:, :LANES]
        for q in range(1, wide):
            total = total + weight[:, q * LANES : (q + 1) * LANES]
        pair = jnp.concatenate([kern.astype(jnp.bfloat16), weight.astype(jnp.bfloat16)], axis=1)
        mixed = jnp.dot(
            pair, jnp.concatenate([ss, xs], axis=0), preferred_element_type=jnp.float32
        )
        if not fresh:
            mixed, total = mixed + acc[i], total + tot[i]
        return mixed, total

    def compute(g, tiles):
        loaded = sources(*GROUPS[g])
        for i in tiles:
            mixed, total = tile_terms(loaded, i, fresh=g == 0)
            acc[i] = mixed
            tot[i] = total

    def start(*some):
        for copy in some:
            copy.start()

    def landed(*some):
        for copy in some:
            copy.wait_recv()

    pl.semaphore_wait(barrier, len(near))
    start(upper[3, 0, 0], upper[1, 0, 1], lower[0, 1], lower[0, 3])
    start(upper[3, 0, 1], upper[1, 0, 0])
    start(x_copies[0, 1])
    for t in (1, 3):
        start(x_copies[t, 0], x_copies[t, 1])
    start(upper[0, 1], upper[0, 3], lower[1, 0], lower[3, 0])
    start(x_copies[2, 0], x_copies[2, 1])

    landed(upper[3, 0, 0])
    start(upper[2, 0, 0])
    landed(upper[1, 0, 1])
    start(upper[2, 0, 1])
    landed(lower[0, 1], lower[0, 3])
    start(lower[0, 2])
    start(*(lower[f, s] for s in (1, 3) for f in (1, 3)))
    landed(upper[3, 0, 1], upper[1, 0, 0])
    start(*(upper[f, s] for f in (1, 3) for s in (1, 3)))
    landed(x_copies[0, 1])
    target_base(0)
    for i, t in ((1, 1), (2, 3)):
        landed(x_copies[t, 0], x_copies[t, 1])
        target_base(i)
    landed(lower[1, 0], lower[3, 0])
    start(lower[2, 0])
    compute(0, (0, 1, 2))

    landed(upper[2, 0, 0])
    start(upper[2, 3, 0], upper[2, 1, 0])
    landed(upper[2, 0, 1])
    start(upper[2, 1, 1], upper[2, 3, 1])
    landed(upper[0, 3], upper[0, 1])
    start(upper[0, 2, 0], upper[0, 2, 1])
    landed(lower[0, 2])
    start(lower[1, 2], lower[3, 2])
    landed(x_copies[2, 0], x_copies[2, 1])
    target_base(3)
    compute(0, (3,))
    landed(lower[2, 0])
    compute(1, (0, 1))

    landed(lower[1, 1], lower[3, 1], lower[1, 3], lower[3, 3])
    start(lower[2, 1], lower[2, 3])
    compute(1, (2, 3))

    landed(upper[1, 1], upper[1, 3])
    start(upper[1, 2, 0], upper[1, 2, 1])
    landed(upper[3, 1], upper[3, 3])
    start(upper[3, 2, 0], upper[3, 2, 1])
    compute(2, (0, 1))

    landed(upper[2, 3, 0])
    start(upper[2, 2, 0])
    landed(upper[2, 1, 1])
    start(upper[2, 2, 1])
    landed(lower[1, 2], lower[3, 2])
    start(lower[2, 2])
    compute(2, (2, 3))

    landed(upper[0, 2, 0], upper[0, 2, 1], upper[2, 1, 0], upper[2, 3, 1], lower[2, 1], lower[2, 3])
    compute(3, (0, 1, 2, 3))
    for f in (1, 3, 2):
        landed(upper[f, 2, 0], upper[f, 2, 1])
    landed(lower[2, 2])

    loaded = sources(*GROUPS[4])
    for i in (3, 1, 2, 0):
        mixed, total = tile_terms(loaded, i)
        total = jnp.sum(total, axis=1, keepdims=True)
        mixed = mixed - tile_points(i).astype(jnp.float32) * total
        for k in range(2):
            n = 2 * i + k
            rows = slice(k * ROWS, (k + 1) * ROWS)
            line = jnp.broadcast_to(total[rows], (ROWS, LANES))
            line = jnp.concatenate([line, line[LANES:]], axis=0).T
            ptot[n] = line[0:1]
            if n == 0:
                acc[0, :ROWS, :] = mixed[rows]
                continue
            for p in range(2):
                part[n, p * ROWS : (p + 1) * ROWS, :] = mixed[
                    rows, p * LANES : (p + 1) * LANES
                ].astype(jnp.bfloat16)
            t = (RING - OFFSETS[i]) % RING
            r_copies[t, k].start()
            p_copies[t, k].start()

    image = acc[0, :ROWS, :]
    totals = ptot[0]
    for t in (0, 1, 3, 2):
        for k in range(2):
            if (t, k) == (0, 0):
                continue
            n = target_slot(t, k)
            r_copies[t, k].wait_recv()
            p_copies[t, k].wait_recv()
            image = image + jnp.concatenate([rsb[n, :ROWS, :], rsb[n, ROWS:, :]], axis=1).astype(jnp.float32)
            totals = totals + rst[n]
    for arrival in arrivals[4:]:
        arrival.wait()
    dg, rg = dg_ref[...], rg_ref[...]
    dv, rv = dv_ref[...], rv_ref[...]
    image = jnp.sqrt(scale_ref[...]) * image + NUGGET * dg
    image_vals = totals[:, :ROWS] + NUGGET * dv

    vals_ref[...] = image_vals
    image_ref[...] = image
    stores = [
        pltpu.make_async_copy(vals_ref, vals_hbm, loads.at[1]),
        pltpu.make_async_copy(image_ref, image_hbm, loads.at[2]),
    ]
    for store in stores:
        store.start()

    def inner(vals, grads):
        first_part = jnp.sum(jnp.sum(grads, axis=0, keepdims=True), axis=1, keepdims=True)
        return first_part + jnp.sum(vals, axis=1, keepdims=True)

    sums = (
        inner(rv * rv, rg * rg),
        inner(dv * image_vals, dg * image),
        inner(rv * image_vals, rg * image),
        inner(image_vals * image_vals, image * image),
    )
    lane_row = lax.broadcasted_iota(jnp.int32, (1, LANES), 1)
    packed = jnp.zeros((1, LANES), jnp.float32)
    for i, value in enumerate(sums):
        packed = jnp.where(lane_row == i, value, packed)
    mine[...] = packed

    me = row * 8 + col

    def spread(i, carry):
        peer = (me + i) % COUNT
        pltpu.make_async_remote_copy(
            src_ref=mine,
            dst_ref=arb.at[me],
            send_sem=a_send,
            recv_sem=a_recv,
            device_id=(peer // 8, peer % 8),
            device_id_type=MESH,
        ).start()
        return carry

    lax.fori_loop(1, COUNT, spread, 0)
    arb[me] = packed
    others = arb.at[pl.ds(0, COUNT - 1)]
    pltpu.make_async_copy(others, others, a_recv).wait()

    every = jnp.sum(arb[...], axis=0)

    def pick(i):
        return jnp.sum(jnp.where(lane_row == i, every, 0.0), axis=1, keepdims=True)

    norm_now, curvature, cross, image_norm = (pick(i) for i in range(4))
    step = norm_now / curvature
    norm_next = norm_now - 2.0 * (step * cross) + step * (step * image_norm)
    ratio = norm_next / norm_now
    pltpu.make_async_copy(others, others, a_send).wait()
    mine[...] = jnp.where(lane_row == 0, step, ratio)
    last = pltpu.make_async_copy(mine, steps_hbm, loads.at[0])
    last.start()

    for group in (upper, lower, x_copies, r_copies, p_copies):
        for copy in group.values():
            copy.wait_send()
    for store in stores:
        store.wait()
    last.wait()


def update(*refs):
    sources, results, held = refs[:9], refs[9:15], refs[15:29]
    steps, arrived, left = refs[29:]
    landing = held[:8] + (steps,)
    loads = [pltpu.make_async_copy(a, b, arrived.at[i]) for i, (a, b) in enumerate(zip(sources, landing))]
    for load in loads:
        load.start()
    for load in loads:
        load.wait()
    sv, sg, rv, rg, dv, dg, iv, ig = (ref[...] for ref in landing[:8])
    step, ratio = steps[:, 0:1], steps[:, 1:2]
    nrv, nrg = rv - step * iv, rg - step * ig
    values = (sv + step * dv, sg + step * dg, nrv, nrg, nrv + ratio * dv, nrg + ratio * dg)
    stores = []
    for i, value in enumerate(values):
        held[8 + i][...] = value
        stores.append(pltpu.make_async_copy(held[8 + i], results[i], left.at[i]))
        stores[i].start()
    for store in stores:
        store.wait()


def body(points, lengthscale, sv, sg, rv, rg, dv, dg):
    hbm = pl.BlockSpec(memory_space=pltpu.HBM)
    line = jax.ShapeDtypeStruct((1, ROWS), jnp.float32)
    block = jax.ShapeDtypeStruct((ROWS, DIM), jnp.float32)
    dma = pltpu.SemaphoreType.DMA
    image_vals, image_grads, steps = pl.pallas_call(
        kernel,
        out_shape=(line, block, jax.ShapeDtypeStruct((1, LANES), jnp.float32)),
        in_specs=[hbm] * 6,
        out_specs=(hbm,) * 3,
        scratch_shapes=[
            pltpu.VMEM((1, ROWS), jnp.float32),
            pltpu.VMEM((ROWS, DIM), jnp.float32),
            pltpu.VMEM((ROWS, DIM), jnp.bfloat16),
            pltpu.VMEM((1, DIM), jnp.float32),
            pltpu.VMEM((1, ROWS), jnp.float32),
            pltpu.VMEM((ROWS, DIM), jnp.float32),
            pltpu.VMEM((1, ROWS), jnp.float32),
            pltpu.VMEM((ROWS, DIM), jnp.float32),
            pltpu.VMEM((16, BLOCK, LANES), jnp.bfloat16),
            pltpu.VMEM((8, X_ROWS, LANES), jnp.bfloat16),
            pltpu.VMEM((4, 2 * ROWS, LANES), jnp.float32),
            pltpu.VMEM((4, 2 * ROWS, DIM), jnp.float32),
            pltpu.VMEM((4, 2 * ROWS, LANES), jnp.float32),
            pltpu.VMEM((8, X_ROWS, LANES), jnp.bfloat16),
            pltpu.VMEM((8, 1, 2 * LANES), jnp.float32),
            pltpu.VMEM((8, X_ROWS, LANES), jnp.bfloat16),
            pltpu.VMEM((8, 1, 2 * LANES), jnp.float32),
            pltpu.VMEM((16, LANES), jnp.float32),
            pltpu.VMEM((1, LANES), jnp.float32),
            pltpu.VMEM((COUNT, 1, LANES), jnp.float32),
            dma((39,)),
            dma((39,)),
            dma((8,)),
            dma((8,)),
            dma((8,)),
            dma((8,)),
            dma((8,)),
            dma((8,)),
            dma,
            dma,
            dma((6,)),
        ],
        compiler_params=pltpu.CompilerParams(
            collective_id=0, has_side_effects=True, vmem_limit_bytes=GRANT
        ),
        cost_estimate=pl.CostEstimate(
            flops=9_700_000_000, bytes_accessed=2_000_000, transcendentals=4_800_000
        ),
    )(
        points,
        lengthscale.reshape(1, DIM),
        rv.reshape(1, ROWS),
        rg,
        dv.reshape(1, ROWS),
        dg,
    )
    nsv, nsg, nrv, nrg, ndv, ndg = pl.pallas_call(
        update,
        out_shape=(line, block) * 3,
        in_specs=[hbm] * 9,
        out_specs=(hbm,) * 6,
        scratch_shapes=[pltpu.VMEM((1, ROWS), jnp.float32), pltpu.VMEM((ROWS, DIM), jnp.float32)] * 7
        + [pltpu.VMEM((1, LANES), jnp.float32), dma((9,)), dma((6,))],
        compiler_params=pltpu.CompilerParams(vmem_limit_bytes=GRANT),
    )(
        sv.reshape(1, ROWS),
        sg,
        rv.reshape(1, ROWS),
        rg,
        dv.reshape(1, ROWS),
        dg,
        image_vals,
        image_grads,
        steps,
    )
    return (nsv.reshape(ROWS), nsg, nrv.reshape(ROWS), nrg, ndv.reshape(ROWS), ndg)


def solution(mesh):
    lines, blocks = P(("row", "col")), P(("row", "col"), None)
    return jax.shard_map(
        body,
        mesh=mesh,
        in_specs=(blocks, P(), lines, blocks, lines, blocks, lines, blocks),
        out_specs=(lines, blocks) * 3,
        check_vma=False,
    )
```

```python
import functools
import math

import jax
import jax.numpy as jnp
from jax import lax
from jax.experimental import pallas as pl
from jax.experimental.pallas import tpu as pltpu
from jax.sharding import PartitionSpec as P

MESH = pl.DeviceIdType.MESH
LOG2E = math.log2(math.e)
NUGGET = 4.0
RING = 4
ROWS = 192
DIM = 256
LANES = 128
TAIL = ROWS - LANES
X_ROWS = 2 * ROWS
PLANES = (0, ROWS, 2 * ROWS, 3 * ROWS + 16)
VECTORS = slice(3 * ROWS, 3 * ROWS + 16)
BLOCK = 4 * ROWS + 16
SPLIT = 656
CUT = 320
OFFSETS = (0, 1, 3, 2)
COUNT = 128
GRANT = 62 << 20
ORDER = (
    ((0, 0), (1, 0), (3, 0))
    + ((0, 1), (0, 3), (2, 0))
    + ((1, 1), (1, 3), (3, 1), (3, 3))
    + ((0, 2), (2, 1), (2, 3))
    + ((1, 2), (3, 2), (2, 2))
)
GROUPS = (
    ((0, 1, 2), (0, 1)),
    ((3, 4, 5), (2, 3, 4, 5)),
    ((6, 7, 8, 9), (6, 7, 8, 9)),
    ((10, 11, 12), (10, 11)),
    ((13, 14, 15), (12, 13, 14, 15)),
)


def slot_of(f, s):
    return ORDER.index((f, s))


def target_slot(t, k):
    return 2 * OFFSETS.index(t % RING) + k


def kernel(
    points_hbm,
    scale_hbm,
    rv_hbm,
    rg_hbm,
    dv_hbm,
    dg_hbm,
    vals_hbm,
    image_hbm,
    steps_hbm,
    vals_ref,
    image_ref,
    points_ref,
    scale_ref,
    rv_ref,
    rg_ref,
    dv_ref,
    dg_ref,
    slots,
    tx,
    ta,
    acc,
    tot,
    part,
    ptot,
    rsb,
    rst,
    vecs,
    mine,
    arb,
    g_send,
    g_recv,
    x_send,
    x_recv,
    r_send,
    r_recv,
    p_send,
    p_recv,
    a_send,
    a_recv,
    loads,
):
    row, col = lax.axis_index("row"), lax.axis_index("col")
    z, y = lax.div(row, RING), lax.rem(row, RING)
    x, c = lax.div(col, 2), lax.rem(col, 2)
    o = 1 - c

    def turn(place, d):
        return lax.rem(place + d, RING)

    def first(d):
        return (z * RING + turn(y, d), col)

    def second(d, core):
        return (turn(z, o * d) * RING + y, turn(x, c * d) * 2 + core)

    def third(d, core):
        return (turn(z, c * d) * RING + y, turn(x, o * d) * 2 + core)

    pairs = (
        (points_hbm, points_ref),
        (scale_hbm, scale_ref),
        (dg_hbm, dg_ref),
        (dv_hbm, dv_ref),
        (rg_hbm, rg_ref),
        (rv_hbm, rv_ref),
    )
    arrivals = [pltpu.make_async_copy(a, b, loads.at[i]) for i, (a, b) in enumerate(pairs)]
    for arrival in arrivals:
        arrival.start()

    barrier = pltpu.get_barrier_semaphore()
    near = [first(1), first(3), second(1, c), second(3, c)]
    near += [third(t, c) for t in (1, 2, 3)] + [third(t, o) for t in range(RING)]
    near += [second(t, o) for t in (1, 2, 3)]
    for peer in near:
        pl.semaphore_signal(barrier, inc=1, device_id=peer, device_id_type=MESH)

    for arrival in arrivals[:4]:
        arrival.wait()

    root = jnp.sqrt(scale_ref[...])
    scaled = (points_ref[...].astype(jnp.float32) * root).astype(jnp.bfloat16)
    slope = (dg_ref[...] * root).astype(jnp.bfloat16)
    for p in range(2):
        lanes = slice(p * LANES, (p + 1) * LANES)
        slots[0, p * ROWS : (p + 1) * ROWS, :] = scaled[:, lanes]
        slots[0, PLANES[2 + p] : PLANES[2 + p] + ROWS, :] = slope[:, lanes]
        tx[0, p * ROWS : (p + 1) * ROWS, :] = scaled[:, lanes]
    wide = scaled.astype(jnp.float32)
    square = jnp.sum(wide * wide, axis=1, keepdims=True)
    shift = jnp.sum(wide * slope.astype(jnp.float32), axis=1, keepdims=True)
    lane = lax.broadcasted_iota(jnp.int32, (ROWS, LANES), 1)
    both = jnp.where(lane == 0, square, jnp.where(lane == 1, shift, 0.0))
    both = jnp.concatenate([both, both[LANES:]], axis=0)
    across = both.T
    level = dv_ref[...].astype(jnp.bfloat16).astype(jnp.float32)
    base = across[0:1] * (-0.5 * LOG2E)
    terms = (
        base[:, :LANES],
        base[:, LANES:],
        level[:, :LANES] - across[1:2, :LANES],
        jnp.concatenate([level[:, LANES:], level[:, LANES:]], axis=1) - across[1:2, LANES:],
    )
    vecs[...] = jnp.zeros_like(vecs)
    for i, term in enumerate(terms):
        for j in range(3):
            piece = term.astype(jnp.bfloat16).astype(jnp.float32)
            vecs[3 * i + j : 3 * i + j + 1, :] = piece
            term = term - piece
    slots[0, VECTORS, :] = vecs[...].astype(jnp.bfloat16)

    upper, lower = {}, {}

    def describe(group, key, slot, source, top, stop, peer):
        n = len(upper) + len(lower)
        group[key] = pltpu.make_async_remote_copy(
            src_ref=slots.at[source, pl.ds(top, stop - top)],
            dst_ref=slots.at[slot, pl.ds(top, stop - top)],
            send_sem=g_send.at[n],
            recv_sem=g_recv.at[n],
            device_id=peer,
            device_id_type=MESH,
        )

    def pieces(f, s, source, peer):
        describe(upper, (f, s, 0), slot_of(f, s), slot_of(*source), 0, CUT, peer)
        describe(upper, (f, s, 1), slot_of(f, s), slot_of(*source), CUT, SPLIT, peer)

    def whole(f, s, source, peer):
        describe(upper, (f, s), slot_of(f, s), slot_of(*source), 0, SPLIT, peer)

    def halves(f, s, behind, ahead, forward, back):
        describe(upper, (f, s, 0), slot_of(f, s), slot_of(*behind), 0, CUT, forward)
        describe(upper, (f, s, 1), slot_of(f, s), slot_of(*ahead), CUT, SPLIT, back)

    pieces(1, 0, (0, 0), first(3))
    pieces(3, 0, (0, 0), first(1))
    halves(2, 0, (3, 0), (1, 0), first(1), first(3))
    for f in OFFSETS:
        cast = pieces if f == 2 else whole
        cast(f, 1, (f, 0), second(3, c))
        cast(f, 3, (f, 0), second(1, c))
        halves(f, 2, (f, 3), (f, 1), second(1, c), second(3, c))

    def other(f, s, source, peer):
        describe(lower, (f, s), slot_of(f, s), source, SPLIT, BLOCK, peer)

    def across_core(behind, ahead):
        return slot_of(*behind) * o + slot_of(*ahead) * c

    away = 1 + 2 * c
    other(0, 1, slot_of(0, 0), second(3, c))
    other(0, 3, slot_of(0, 0), second(1, c))
    other(0, 2, across_core((0, 3), (0, 1)), second(away, c))
    for s in OFFSETS:
        other(1, s, slot_of(0, s), first(3))
        other(3, s, slot_of(0, s), first(1))
        other(2, s, across_core((3, s), (1, s)), first(away))

    x_copies, r_copies, p_copies = {}, {}, {}
    for t in OFFSETS:
        for k in range(2):
            if (t, k) == (0, 0):
                continue
            n = target_slot(t, k)
            back = (RING - t) % RING
            x_copies[t, k] = pltpu.make_async_remote_copy(
                src_ref=slots.at[0, pl.ds(0, X_ROWS)],
                dst_ref=tx.at[n],
                send_sem=x_send.at[n],
                recv_sem=x_recv.at[n],
                device_id=second(back, o) if k else third(back, c),
                device_id_type=MESH,
            )
            owner = third(back, o) if k else third(back, c)
            r_copies[t, k] = pltpu.make_async_remote_copy(
                src_ref=part.at[target_slot(back, k)],
                dst_ref=rsb.at[n],
                send_sem=r_send.at[n],
                recv_sem=r_recv.at[n],
                device_id=owner,
                device_id_type=MESH,
            )
            p_copies[t, k] = pltpu.make_async_remote_copy(
                src_ref=ptot.at[target_slot(back, k)],
                dst_ref=rst.at[n],
                send_sem=p_send.at[n],
                recv_sem=p_recv.at[n],
                device_id=owner,
                device_id_type=MESH,
            )

    def tile_points(i):
        planes = []
        for p in range(2):
            rows = slice(p * ROWS, (p + 1) * ROWS)
            planes.append(jnp.concatenate([tx[2 * i, rows, :], tx[2 * i + 1, rows, :]], axis=0))
        return jnp.concatenate(planes, axis=1)

    def target_base(i):
        value = tile_points(i).astype(jnp.float32)
        total = jnp.sum(value * value, axis=1, keepdims=True) * (-0.5 * LOG2E)
        ta[i] = jnp.broadcast_to(total, (2 * ROWS, LANES))

    low = lax.broadcasted_iota(jnp.int32, (1, LANES), 1) < TAIL

    def sources(heads, tails):
        def plane(p):
            top = PLANES[p]
            pieces = [slots[s, top : top + LANES, :] for s in heads]
            pieces += [slots[s, top + LANES : top + ROWS, :] for s in tails]
            return jnp.concatenate(pieces, axis=0)

        xs = jnp.concatenate([plane(0), plane(1)], axis=1)
        ss = jnp.concatenate([plane(2), plane(3)], axis=1)

        def vector(i):
            def read(s, j):
                v = slots[s, VECTORS, :].astype(jnp.float32)
                return v[j : j + 1] + v[j + 1 : j + 2] + v[j + 2 : j + 3]

            pieces = [read(s, 3 * i) for s in heads]
            ends = [read(s, 3 * i + 3) for s in tails]
            pieces += [jnp.where(low, u, v) for u, v in zip(ends[::2], ends[1::2])]
            return jnp.concatenate(pieces, axis=1)

        return xs, ss, vector(0), vector(2)

    def contract(left, right):
        return lax.dot_general(
            left, right, (((1,), (1,)), ((), ())), preferred_element_type=jnp.float32
        )

    def tile_terms(loaded, i, fresh=False):
        xs, ss, sb, sc = loaded
        points = tile_points(i)
        wide = xs.shape[0] // LANES
        base = jnp.concatenate([ta[i]] * wide, axis=1)
        kern = jnp.exp2(contract(points, xs) * LOG2E + (base + sb))
        weight = kern * (contract(points, ss) + sc)
        total = weight[:, :LANES]
        for q in range(1, wide):
            total = total + weight[:, q * LANES : (q + 1) * LANES]
        pair = jnp.concatenate([kern.astype(jnp.bfloat16), weight.astype(jnp.bfloat16)], axis=1)
        mixed = jnp.dot(
            pair, jnp.concatenate([ss, xs], axis=0), preferred_element_type=jnp.float32
        )
        if not fresh:
            mixed, total = mixed + acc[i], total + tot[i]
        return mixed, total

    def compute(g, tiles):
        loaded = sources(*GROUPS[g])
        for i in tiles:
            mixed, total = tile_terms(loaded, i, fresh=g == 0)
            acc[i] = mixed
            tot[i] = total

    def start(*some):
        for copy in some:
            copy.start()

    def landed(*some):
        for copy in some:
            copy.wait_recv()

    pl.semaphore_wait(barrier, len(near))
    start(upper[3, 0, 0], upper[1, 0, 1], lower[0, 1], lower[0, 3])
    start(upper[3, 0, 1], upper[1, 0, 0])
    start(x_copies[0, 1])
    for t in (1, 3):
        start(x_copies[t, 0], x_copies[t, 1])
    start(upper[0, 1], upper[0, 3], lower[1, 0], lower[3, 0])
    start(x_copies[2, 0], x_copies[2, 1])

    landed(upper[3, 0, 0])
    start(upper[2, 0, 0])
    landed(upper[1, 0, 1])
    start(upper[2, 0, 1])
    landed(lower[0, 1], lower[0, 3])
    start(lower[0, 2])
    start(*(lower[f, s] for s in (1, 3) for f in (1, 3)))
    landed(upper[3, 0, 1], upper[1, 0, 0])
    start(*(upper[f, s] for f in (1, 3) for s in (1, 3)))
    landed(x_copies[0, 1])
    target_base(0)
    for i, t in ((1, 1), (2, 3)):
        landed(x_copies[t, 0], x_copies[t, 1])
        target_base(i)
    landed(lower[1, 0], lower[3, 0])
    start(lower[2, 0])
    compute(0, (0, 1, 2))

    landed(upper[2, 0, 0])
    start(upper[2, 3, 0], upper[2, 1, 0])
    landed(upper[2, 0, 1])
    start(upper[2, 1, 1], upper[2, 3, 1])
    landed(upper[0, 3], upper[0, 1])
    start(upper[0, 2, 0], upper[0, 2, 1])
    landed(lower[0, 2])
    start(lower[1, 2], lower[3, 2])
    landed(x_copies[2, 0], x_copies[2, 1])
    target_base(3)
    compute(0, (3,))
    landed(lower[2, 0])
    compute(1, (0, 1))

    landed(lower[1, 1], lower[3, 1], lower[1, 3], lower[3, 3])
    start(lower[2, 1], lower[2, 3])
    compute(1, (2, 3))

    landed(upper[1, 1], upper[1, 3])
    start(upper[1, 2, 0], upper[1, 2, 1])
    landed(upper[3, 1], upper[3, 3])
    start(upper[3, 2, 0], upper[3, 2, 1])
    compute(2, (0, 1))

    landed(upper[2, 3, 0])
    start(upper[2, 2, 0])
    landed(upper[2, 1, 1])
    start(upper[2, 2, 1])
    landed(lower[1, 2], lower[3, 2])
    start(lower[2, 2])
    compute(2, (2, 3))

    landed(upper[0, 2, 0], upper[0, 2, 1], upper[2, 1, 0], upper[2, 3, 1], lower[2, 1], lower[2, 3])
    compute(3, (0, 1, 2, 3))
    for f in (1, 3, 2):
        landed(upper[f, 2, 0], upper[f, 2, 1])
    landed(lower[2, 2])

    loaded = sources(*GROUPS[4])
    for i in (3, 1, 2, 0):
        mixed, total = tile_terms(loaded, i)
        total = jnp.sum(total, axis=1, keepdims=True)
        mixed = mixed - tile_points(i).astype(jnp.float32) * total
        for k in range(2):
            n = 2 * i + k
            rows = slice(k * ROWS, (k + 1) * ROWS)
            line = jnp.broadcast_to(total[rows], (ROWS, LANES))
            line = jnp.concatenate([line, line[LANES:]], axis=0).T
            ptot[n] = line[0:1]
            if n == 0:
                acc[0, :ROWS, :] = mixed[rows]
                continue
            for p in range(2):
                part[n, p * ROWS : (p + 1) * ROWS, :] = mixed[
                    rows, p * LANES : (p + 1) * LANES
                ].astype(jnp.bfloat16)
            t = (RING - OFFSETS[i]) % RING
            r_copies[t, k].start()
            p_copies[t, k].start()

    image = acc[0, :ROWS, :]
    totals = ptot[0]
    for t in (0, 1, 3, 2):
        for k in range(2):
            if (t, k) == (0, 0):
                continue
            n = target_slot(t, k)
            r_copies[t, k].wait_recv()
            p_copies[t, k].wait_recv()
            image = image + jnp.concatenate([rsb[n, :ROWS, :], rsb[n, ROWS:, :]], axis=1).astype(jnp.float32)
            totals = totals + rst[n]
    for arrival in arrivals[4:]:
        arrival.wait()
    dg, rg = dg_ref[...], rg_ref[...]
    dv, rv = dv_ref[...], rv_ref[...]
    image = jnp.sqrt(scale_ref[...]) * image + NUGGET * dg
    image_vals = totals[:, :ROWS] + NUGGET * dv

    vals_ref[...] = image_vals
    image_ref[...] = image
    stores = [
        pltpu.make_async_copy(vals_ref, vals_hbm, loads.at[1]),
        pltpu.make_async_copy(image_ref, image_hbm, loads.at[2]),
    ]
    for store in stores:
        store.start()

    def inner(vals, grads):
        first_part = jnp.sum(jnp.sum(grads, axis=0, keepdims=True), axis=1, keepdims=True)
        return first_part + jnp.sum(vals, axis=1, keepdims=True)

    sums = (
        inner(rv * rv, rg * rg),
        inner(dv * image_vals, dg * image),
        inner(rv * image_vals, rg * image),
        inner(image_vals * image_vals, image * image),
    )
    lane_row = lax.broadcasted_iota(jnp.int32, (1, LANES), 1)
    packed = jnp.zeros((1, LANES), jnp.float32)
    for i, value in enumerate(sums):
        packed = jnp.where(lane_row == i, value, packed)
    mine[...] = packed

    me = row * 8 + col

    def spread(i, carry):
        peer = lax.rem(me + i, COUNT)
        pltpu.make_async_remote_copy(
            src_ref=mine,
            dst_ref=arb.at[me],
            send_sem=a_send,
            recv_sem=a_recv,
            device_id=(lax.div(peer, 8), lax.rem(peer, 8)),
            device_id_type=MESH,
        ).start()
        return carry

    lax.fori_loop(1, COUNT, spread, 0)
    arb[me] = packed
    others = arb.at[pl.ds(0, COUNT - 1)]
    pltpu.make_async_copy(others, others, a_recv).wait()

    every = jnp.sum(arb[...], axis=0)

    def pick(i):
        return jnp.sum(jnp.where(lane_row == i, every, 0.0), axis=1, keepdims=True)

    norm_now, curvature, cross, image_norm = (pick(i) for i in range(4))
    step = norm_now / curvature
    norm_next = norm_now - 2.0 * (step * cross) + step * (step * image_norm)
    ratio = norm_next / norm_now
    pltpu.make_async_copy(others, others, a_send).wait()
    mine[...] = jnp.where(lane_row == 0, step, ratio)
    last = pltpu.make_async_copy(mine, steps_hbm, loads.at[0])
    last.start()

    for group in (upper, lower, x_copies, r_copies, p_copies):
        for copy in group.values():
            copy.wait_send()
    for store in stores:
        store.wait()
    last.wait()


def update(*refs):
    sources, results, held = refs[:9], refs[9:15], refs[15:29]
    steps, arrived, left = refs[29:]
    landing = held[:8] + (steps,)
    loads = [pltpu.make_async_copy(a, b, arrived.at[i]) for i, (a, b) in enumerate(zip(sources, landing))]
    for load in loads:
        load.start()
    for load in loads:
        load.wait()
    sv, sg, rv, rg, dv, dg, iv, ig = (ref[...] for ref in landing[:8])
    step, ratio = steps[:, 0:1], steps[:, 1:2]
    nrv, nrg = rv - step * iv, rg - step * ig
    values = (sv + step * dv, sg + step * dg, nrv, nrg, nrv + ratio * dv, nrg + ratio * dg)
    stores = []
    for i, value in enumerate(values):
        held[8 + i][...] = value
        stores.append(pltpu.make_async_copy(held[8 + i], results[i], left.at[i]))
        stores[i].start()
    for store in stores:
        store.wait()


def body(points, lengthscale, sv, sg, rv, rg, dv, dg):
    hbm = pl.BlockSpec(memory_space=pltpu.HBM)
    line = jax.ShapeDtypeStruct((1, ROWS), jnp.float32)
    block = jax.ShapeDtypeStruct((ROWS, DIM), jnp.float32)
    dma = pltpu.SemaphoreType.DMA
    image_vals, image_grads, steps = pl.pallas_call(
        kernel,
        out_shape=(line, block, jax.ShapeDtypeStruct((1, LANES), jnp.float32)),
        in_specs=[hbm] * 6,
        out_specs=(hbm,) * 3,
        scratch_shapes=[
            pltpu.VMEM((1, ROWS), jnp.float32),
            pltpu.VMEM((ROWS, DIM), jnp.float32),
            pltpu.VMEM((ROWS, DIM), jnp.bfloat16),
            pltpu.VMEM((1, DIM), jnp.float32),
            pltpu.VMEM((1, ROWS), jnp.float32),
            pltpu.VMEM((ROWS, DIM), jnp.float32),
            pltpu.VMEM((1, ROWS), jnp.float32),
            pltpu.VMEM((ROWS, DIM), jnp.float32),
            pltpu.VMEM((16, BLOCK, LANES), jnp.bfloat16),
            pltpu.VMEM((8, X_ROWS, LANES), jnp.bfloat16),
            pltpu.VMEM((4, 2 * ROWS, LANES), jnp.float32),
            pltpu.VMEM((4, 2 * ROWS, DIM), jnp.float32),
            pltpu.VMEM((4, 2 * ROWS, LANES), jnp.float32),
            pltpu.VMEM((8, X_ROWS, LANES), jnp.bfloat16),
            pltpu.VMEM((8, 1, 2 * LANES), jnp.float32),
            pltpu.VMEM((8, X_ROWS, LANES), jnp.bfloat16),
            pltpu.VMEM((8, 1, 2 * LANES), jnp.float32),
            pltpu.VMEM((16, LANES), jnp.float32),
            pltpu.VMEM((1, LANES), jnp.float32),
            pltpu.VMEM((COUNT, 1, LANES), jnp.float32),
            dma((39,)),
            dma((39,)),
            dma((8,)),
            dma((8,)),
            dma((8,)),
            dma((8,)),
            dma((8,)),
            dma((8,)),
            dma,
            dma,
            dma((6,)),
        ],
        compiler_params=pltpu.CompilerParams(
            collective_id=0, has_side_effects=True, vmem_limit_bytes=GRANT
        ),
        cost_estimate=pl.CostEstimate(
            flops=9_700_000_000, bytes_accessed=2_000_000, transcendentals=4_800_000
        ),
    )(
        points,
        lengthscale.reshape(1, DIM),
        rv.reshape(1, ROWS),
        rg,
        dv.reshape(1, ROWS),
        dg,
    )
    nsv, nsg, nrv, nrg, ndv, ndg = pl.pallas_call(
        update,
        out_shape=(line, block) * 3,
        in_specs=[hbm] * 9,
        out_specs=(hbm,) * 6,
        scratch_shapes=[pltpu.VMEM((1, ROWS), jnp.float32), pltpu.VMEM((ROWS, DIM), jnp.float32)] * 7
        + [pltpu.VMEM((1, LANES), jnp.float32), dma((9,)), dma((6,))],
        compiler_params=pltpu.CompilerParams(vmem_limit_bytes=GRANT),
    )(
        sv.reshape(1, ROWS),
        sg,
        rv.reshape(1, ROWS),
        rg,
        dv.reshape(1, ROWS),
        dg,
        image_vals,
        image_grads,
        steps,
    )
    return (nsv.reshape(ROWS), nsg, nrv.reshape(ROWS), nrg, ndv.reshape(ROWS), ndg)


def solution(mesh):
    lines, blocks = P(("row", "col")), P(("row", "col"), None)
    return jax.shard_map(
        body,
        mesh=mesh,
        in_specs=(blocks, P(), lines, blocks, lines, blocks, lines, blocks),
        out_specs=(lines, blocks) * 3,
        check_vma=False,
    )
```

```python
import functools
import math

import jax
import jax.numpy as jnp
from jax import lax
from jax.experimental import pallas as pl
from jax.experimental.pallas import tpu as pltpu
from jax.sharding import PartitionSpec as P

MESH = pl.DeviceIdType.MESH
LOG2E = math.log2(math.e)
NUGGET = 4.0
RING = 4
ROWS = 192
DIM = 256
LANES = 128
TAIL = ROWS - LANES
X_ROWS = 2 * ROWS
PLANES = (0, ROWS, 2 * ROWS, 3 * ROWS + 16)
VECTORS = slice(3 * ROWS, 3 * ROWS + 16)
BLOCK = 4 * ROWS + 16
SPLIT = 688
CUT = 336
OFFSETS = (0, 1, 3, 2)
COUNT = 128
GRANT = 62 << 20
ORDER = (
    ((0, 0), (1, 0), (3, 0))
    + ((0, 1), (0, 3), (2, 0))
    + ((1, 1), (1, 3), (3, 1), (3, 3))
    + ((0, 2), (2, 1), (2, 3))
    + ((1, 2), (3, 2), (2, 2))
)
GROUPS = (
    ((0, 1, 2), (0, 1)),
    ((3, 4, 5), (2, 3, 4, 5)),
    ((6, 7, 8, 9), (6, 7, 8, 9)),
    ((10, 11, 12), (10, 11)),
    ((13, 14, 15), (12, 13, 14, 15)),
)


def slot_of(f, s):
    return ORDER.index((f, s))


def target_slot(t, k):
    return 2 * OFFSETS.index(t % RING) + k


def kernel(
    points_hbm,
    scale_hbm,
    rv_hbm,
    rg_hbm,
    dv_hbm,
    dg_hbm,
    vals_hbm,
    image_hbm,
    steps_hbm,
    vals_ref,
    image_ref,
    points_ref,
    scale_ref,
    rv_ref,
    rg_ref,
    dv_ref,
    dg_ref,
    slots,
    tx,
    ta,
    acc,
    tot,
    part,
    ptot,
    rsb,
    rst,
    vecs,
    mine,
    arb,
    g_send,
    g_recv,
    x_send,
    x_recv,
    r_send,
    r_recv,
    p_send,
    p_recv,
    a_send,
    a_recv,
    loads,
):
    row, col = lax.axis_index("row"), lax.axis_index("col")
    z, y = lax.div(row, RING), lax.rem(row, RING)
    x, c = lax.div(col, 2), lax.rem(col, 2)
    o = 1 - c

    def turn(place, d):
        return lax.rem(place + d, RING)

    def first(d):
        return (z * RING + turn(y, d), col)

    def second(d, core):
        return (turn(z, o * d) * RING + y, turn(x, c * d) * 2 + core)

    def third(d, core):
        return (turn(z, c * d) * RING + y, turn(x, o * d) * 2 + core)

    pairs = (
        (points_hbm, points_ref),
        (scale_hbm, scale_ref),
        (dg_hbm, dg_ref),
        (dv_hbm, dv_ref),
        (rg_hbm, rg_ref),
        (rv_hbm, rv_ref),
    )
    arrivals = [pltpu.make_async_copy(a, b, loads.at[i]) for i, (a, b) in enumerate(pairs)]
    for arrival in arrivals:
        arrival.start()

    barrier = pltpu.get_barrier_semaphore()
    near = [first(1), first(3), second(1, c), second(3, c)]
    near += [third(t, c) for t in (1, 2, 3)] + [third(t, o) for t in range(RING)]
    near += [second(t, o) for t in (1, 2, 3)]
    for peer in near:
        pl.semaphore_signal(barrier, inc=1, device_id=peer, device_id_type=MESH)

    for arrival in arrivals[:4]:
        arrival.wait()

    root = jnp.sqrt(scale_ref[...])
    scaled = (points_ref[...].astype(jnp.float32) * root).astype(jnp.bfloat16)
    slope = (dg_ref[...] * root).astype(jnp.bfloat16)
    for p in range(2):
        lanes = slice(p * LANES, (p + 1) * LANES)
        slots[0, p * ROWS : (p + 1) * ROWS, :] = scaled[:, lanes]
        slots[0, PLANES[2 + p] : PLANES[2 + p] + ROWS, :] = slope[:, lanes]
        tx[0, p * ROWS : (p + 1) * ROWS, :] = scaled[:, lanes]
    wide = scaled.astype(jnp.float32)
    square = jnp.sum(wide * wide, axis=1, keepdims=True)
    shift = jnp.sum(wide * slope.astype(jnp.float32), axis=1, keepdims=True)
    lane = lax.broadcasted_iota(jnp.int32, (ROWS, LANES), 1)
    both = jnp.where(lane == 0, square, jnp.where(lane == 1, shift, 0.0))
    both = jnp.concatenate([both, both[LANES:]], axis=0)
    across = both.T
    level = dv_ref[...].astype(jnp.bfloat16).astype(jnp.float32)
    base = across[0:1] * (-0.5 * LOG2E)
    terms = (
        base[:, :LANES],
        base[:, LANES:],
        level[:, :LANES] - across[1:2, :LANES],
        jnp.concatenate([level[:, LANES:], level[:, LANES:]], axis=1) - across[1:2, LANES:],
    )
    vecs[...] = jnp.zeros_like(vecs)
    for i, term in enumerate(terms):
        for j in range(3):
            piece = term.astype(jnp.bfloat16).astype(jnp.float32)
            vecs[3 * i + j : 3 * i + j + 1, :] = piece
            term = term - piece
    slots[0, VECTORS, :] = vecs[...].astype(jnp.bfloat16)

    upper, lower = {}, {}

    def describe(group, key, slot, source, top, stop, peer):
        n = len(upper) + len(lower)
        group[key] = pltpu.make_async_remote_copy(
            src_ref=slots.at[source, pl.ds(top, stop - top)],
            dst_ref=slots.at[slot, pl.ds(top, stop - top)],
            send_sem=g_send.at[n],
            recv_sem=g_recv.at[n],
            device_id=peer,
            device_id_type=MESH,
        )

    def pieces(f, s, source, peer):
        describe(upper, (f, s, 0), slot_of(f, s), slot_of(*source), 0, CUT, peer)
        describe(upper, (f, s, 1), slot_of(f, s), slot_of(*source), CUT, SPLIT, peer)

    def whole(f, s, source, peer):
        describe(upper, (f, s), slot_of(f, s), slot_of(*source), 0, SPLIT, peer)

    def halves(f, s, behind, ahead, forward, back):
        describe(upper, (f, s, 0), slot_of(f, s), slot_of(*behind), 0, CUT, forward)
        describe(upper, (f, s, 1), slot_of(f, s), slot_of(*ahead), CUT, SPLIT, back)

    pieces(1, 0, (0, 0), first(3))
    pieces(3, 0, (0, 0), first(1))
    halves(2, 0, (3, 0), (1, 0), first(1), first(3))
    for f in OFFSETS:
        cast = pieces if f == 2 else whole
        cast(f, 1, (f, 0), second(3, c))
        cast(f, 3, (f, 0), second(1, c))
        halves(f, 2, (f, 3), (f, 1), second(1, c), second(3, c))

    def other(f, s, source, peer):
        describe(lower, (f, s), slot_of(f, s), source, SPLIT, BLOCK, peer)

    def across_core(behind, ahead):
        return slot_of(*behind) * o + slot_of(*ahead) * c

    away = 1 + 2 * c
    other(0, 1, slot_of(0, 0), second(3, c))
    other(0, 3, slot_of(0, 0), second(1, c))
    other(0, 2, across_core((0, 3), (0, 1)), second(away, c))
    for s in OFFSETS:
        other(1, s, slot_of(0, s), first(3))
        other(3, s, slot_of(0, s), first(1))
        other(2, s, across_core((3, s), (1, s)), first(away))

    x_copies, r_copies, p_copies = {}, {}, {}
    for t in OFFSETS:
        for k in range(2):
            if (t, k) == (0, 0):
                continue
            n = target_slot(t, k)
            back = (RING - t) % RING
            x_copies[t, k] = pltpu.make_async_remote_copy(
                src_ref=slots.at[0, pl.ds(0, X_ROWS)],
                dst_ref=tx.at[n],
                send_sem=x_send.at[n],
                recv_sem=x_recv.at[n],
                device_id=second(back, o) if k else third(back, c),
                device_id_type=MESH,
            )
            owner = third(back, o) if k else third(back, c)
            r_copies[t, k] = pltpu.make_async_remote_copy(
                src_ref=part.at[target_slot(back, k)],
                dst_ref=rsb.at[n],
                send_sem=r_send.at[n],
                recv_sem=r_recv.at[n],
                device_id=owner,
                device_id_type=MESH,
            )
            p_copies[t, k] = pltpu.make_async_remote_copy(
                src_ref=ptot.at[target_slot(back, k)],
                dst_ref=rst.at[n],
                send_sem=p_send.at[n],
                recv_sem=p_recv.at[n],
                device_id=owner,
                device_id_type=MESH,
            )

    def tile_points(i):
        planes = []
        for p in range(2):
            rows = slice(p * ROWS, (p + 1) * ROWS)
            planes.append(jnp.concatenate([tx[2 * i, rows, :], tx[2 * i + 1, rows, :]], axis=0))
        return jnp.concatenate(planes, axis=1)

    def target_base(i):
        value = tile_points(i).astype(jnp.float32)
        total = jnp.sum(value * value, axis=1, keepdims=True) * (-0.5 * LOG2E)
        ta[i] = jnp.broadcast_to(total, (2 * ROWS, LANES))

    low = lax.broadcasted_iota(jnp.int32, (1, LANES), 1) < TAIL

    def sources(heads, tails):
        def plane(p):
            top = PLANES[p]
            pieces = [slots[s, top : top + LANES, :] for s in heads]
            pieces += [slots[s, top + LANES : top + ROWS, :] for s in tails]
            return jnp.concatenate(pieces, axis=0)

        xs = jnp.concatenate([plane(0), plane(1)], axis=1)
        ss = jnp.concatenate([plane(2), plane(3)], axis=1)

        def vector(i):
            def read(s, j):
                v = slots[s, VECTORS, :].astype(jnp.float32)
                return v[j : j + 1] + v[j + 1 : j + 2] + v[j + 2 : j + 3]

            pieces = [read(s, 3 * i) for s in heads]
            ends = [read(s, 3 * i + 3) for s in tails]
            pieces += [jnp.where(low, u, v) for u, v in zip(ends[::2], ends[1::2])]
            return jnp.concatenate(pieces, axis=1)

        return xs, ss, vector(0), vector(2)

    def contract(left, right):
        return lax.dot_general(
            left, right, (((1,), (1,)), ((), ())), preferred_element_type=jnp.float32
        )

    def tile_terms(loaded, i, fresh=False):
        xs, ss, sb, sc = loaded
        points = tile_points(i)
        wide = xs.shape[0] // LANES
        base = jnp.concatenate([ta[i]] * wide, axis=1)
        kern = jnp.exp2(contract(points, xs) * LOG2E + (base + sb))
        weight = kern * (contract(points, ss) + sc)
        total = weight[:, :LANES]
        for q in range(1, wide):
            total = total + weight[:, q * LANES : (q + 1) * LANES]
        pair = jnp.concatenate([kern.astype(jnp.bfloat16), weight.astype(jnp.bfloat16)], axis=1)
        mixed = jnp.dot(
            pair, jnp.concatenate([ss, xs], axis=0), preferred_element_type=jnp.float32
        )
        if not fresh:
            mixed, total = mixed + acc[i], total + tot[i]
        return mixed, total

    def compute(g, tiles):
        loaded = sources(*GROUPS[g])
        for i in tiles:
            mixed, total = tile_terms(loaded, i, fresh=g == 0)
            acc[i] = mixed
            tot[i] = total

    def start(*some):
        for copy in some:
            copy.start()

    def landed(*some):
        for copy in some:
            copy.wait_recv()

    pl.semaphore_wait(barrier, len(near))
    start(upper[3, 0, 0], upper[1, 0, 1], lower[0, 1], lower[0, 3])
    start(upper[3, 0, 1], upper[1, 0, 0])
    start(x_copies[0, 1])
    for t in (1, 3):
        start(x_copies[t, 0], x_copies[t, 1])
    start(upper[0, 1], upper[0, 3], lower[1, 0], lower[3, 0])
    start(x_copies[2, 0], x_copies[2, 1])

    landed(upper[3, 0, 0])
    start(upper[2, 0, 0])
    landed(upper[1, 0, 1])
    start(upper[2, 0, 1])
    landed(lower[0, 1], lower[0, 3])
    start(lower[0, 2])
    start(*(lower[f, s] for s in (1, 3) for f in (1, 3)))
    landed(upper[3, 0, 1], upper[1, 0, 0])
    start(*(upper[f, s] for f in (1, 3) for s in (1, 3)))
    landed(x_copies[0, 1])
    target_base(0)
    for i, t in ((1, 1), (2, 3)):
        landed(x_copies[t, 0], x_copies[t, 1])
        target_base(i)
    landed(lower[1, 0], lower[3, 0])
    start(lower[2, 0])
    compute(0, (0, 1, 2))

    landed(upper[2, 0, 0])
    start(upper[2, 3, 0], upper[2, 1, 0])
    landed(upper[2, 0, 1])
    start(upper[2, 1, 1], upper[2, 3, 1])
    landed(upper[0, 3], upper[0, 1])
    start(upper[0, 2, 0], upper[0, 2, 1])
    landed(lower[0, 2])
    start(lower[1, 2], lower[3, 2])
    landed(x_copies[2, 0], x_copies[2, 1])
    target_base(3)
    compute(0, (3,))
    landed(lower[2, 0])
    compute(1, (0, 1))

    landed(lower[1, 1], lower[3, 1], lower[1, 3], lower[3, 3])
    start(lower[2, 1], lower[2, 3])
    compute(1, (2, 3))

    landed(upper[1, 1], upper[1, 3])
    start(upper[1, 2, 0], upper[1, 2, 1])
    landed(upper[3, 1], upper[3, 3])
    start(upper[3, 2, 0], upper[3, 2, 1])
    compute(2, (0, 1))

    landed(upper[2, 3, 0])
    start(upper[2, 2, 0])
    landed(upper[2, 1, 1])
    start(upper[2, 2, 1])
    landed(lower[1, 2], lower[3, 2])
    start(lower[2, 2])
    compute(2, (2, 3))

    landed(upper[0, 2, 0], upper[0, 2, 1], upper[2, 1, 0], upper[2, 3, 1], lower[2, 1], lower[2, 3])
    compute(3, (0, 1, 2, 3))
    for f in (1, 3, 2):
        landed(upper[f, 2, 0], upper[f, 2, 1])
    landed(lower[2, 2])

    loaded = sources(*GROUPS[4])
    for i in (3, 1, 2, 0):
        mixed, total = tile_terms(loaded, i)
        total = jnp.sum(total, axis=1, keepdims=True)
        mixed = mixed - tile_points(i).astype(jnp.float32) * total
        for k in range(2):
            n = 2 * i + k
            rows = slice(k * ROWS, (k + 1) * ROWS)
            line = jnp.broadcast_to(total[rows], (ROWS, LANES))
            line = jnp.concatenate([line, line[LANES:]], axis=0).T
            ptot[n] = line[0:1]
            if n == 0:
                acc[0, :ROWS, :] = mixed[rows]
                continue
            for p in range(2):
                part[n, p * ROWS : (p + 1) * ROWS, :] = mixed[
                    rows, p * LANES : (p + 1) * LANES
                ].astype(jnp.bfloat16)
            t = (RING - OFFSETS[i]) % RING
            r_copies[t, k].start()
            p_copies[t, k].start()

    image = acc[0, :ROWS, :]
    totals = ptot[0]
    for t in (0, 1, 3, 2):
        for k in range(2):
            if (t, k) == (0, 0):
                continue
            n = target_slot(t, k)
            r_copies[t, k].wait_recv()
            p_copies[t, k].wait_recv()
            image = image + jnp.concatenate([rsb[n, :ROWS, :], rsb[n, ROWS:, :]], axis=1).astype(jnp.float32)
            totals = totals + rst[n]
    for arrival in arrivals[4:]:
        arrival.wait()
    dg, rg = dg_ref[...], rg_ref[...]
    dv, rv = dv_ref[...], rv_ref[...]
    image = jnp.sqrt(scale_ref[...]) * image + NUGGET * dg
    image_vals = totals[:, :ROWS] + NUGGET * dv

    vals_ref[...] = image_vals
    image_ref[...] = image
    stores = [
        pltpu.make_async_copy(vals_ref, vals_hbm, loads.at[1]),
        pltpu.make_async_copy(image_ref, image_hbm, loads.at[2]),
    ]
    for store in stores:
        store.start()

    def inner(vals, grads):
        first_part = jnp.sum(jnp.sum(grads, axis=0, keepdims=True), axis=1, keepdims=True)
        return first_part + jnp.sum(vals, axis=1, keepdims=True)

    sums = (
        inner(rv * rv, rg * rg),
        inner(dv * image_vals, dg * image),
        inner(rv * image_vals, rg * image),
        inner(image_vals * image_vals, image * image),
    )
    lane_row = lax.broadcasted_iota(jnp.int32, (1, LANES), 1)
    packed = jnp.zeros((1, LANES), jnp.float32)
    for i, value in enumerate(sums):
        packed = jnp.where(lane_row == i, value, packed)
    mine[...] = packed

    me = row * 8 + col

    def spread(i, carry):
        peer = lax.rem(me + i, COUNT)
        pltpu.make_async_remote_copy(
            src_ref=mine,
            dst_ref=arb.at[me],
            send_sem=a_send,
            recv_sem=a_recv,
            device_id=(lax.div(peer, 8), lax.rem(peer, 8)),
            device_id_type=MESH,
        ).start()
        return carry

    lax.fori_loop(1, COUNT, spread, 0)
    arb[me] = packed
    others = arb.at[pl.ds(0, COUNT - 1)]
    pltpu.make_async_copy(others, others, a_recv).wait()

    every = jnp.sum(arb[...], axis=0)

    def pick(i):
        return jnp.sum(jnp.where(lane_row == i, every, 0.0), axis=1, keepdims=True)

    norm_now, curvature, cross, image_norm = (pick(i) for i in range(4))
    step = norm_now / curvature
    norm_next = norm_now - 2.0 * (step * cross) + step * (step * image_norm)
    ratio = norm_next / norm_now
    pltpu.make_async_copy(others, others, a_send).wait()
    mine[...] = jnp.where(lane_row == 0, step, ratio)
    last = pltpu.make_async_copy(mine, steps_hbm, loads.at[0])
    last.start()

    for group in (upper, lower, x_copies, r_copies, p_copies):
        for copy in group.values():
            copy.wait_send()
    for store in stores:
        store.wait()
    last.wait()


def update(*refs):
    sources, results, held = refs[:9], refs[9:15], refs[15:29]
    steps, arrived, left = refs[29:]
    landing = held[:8] + (steps,)
    loads = [pltpu.make_async_copy(a, b, arrived.at[i]) for i, (a, b) in enumerate(zip(sources, landing))]
    for load in loads:
        load.start()
    for load in loads:
        load.wait()
    sv, sg, rv, rg, dv, dg, iv, ig = (ref[...] for ref in landing[:8])
    step, ratio = steps[:, 0:1], steps[:, 1:2]
    nrv, nrg = rv - step * iv, rg - step * ig
    values = (sv + step * dv, sg + step * dg, nrv, nrg, nrv + ratio * dv, nrg + ratio * dg)
    stores = []
    for i, value in enumerate(values):
        held[8 + i][...] = value
        stores.append(pltpu.make_async_copy(held[8 + i], results[i], left.at[i]))
        stores[i].start()
    for store in stores:
        store.wait()


def body(points, lengthscale, sv, sg, rv, rg, dv, dg):
    hbm = pl.BlockSpec(memory_space=pltpu.HBM)
    line = jax.ShapeDtypeStruct((1, ROWS), jnp.float32)
    block = jax.ShapeDtypeStruct((ROWS, DIM), jnp.float32)
    dma = pltpu.SemaphoreType.DMA
    image_vals, image_grads, steps = pl.pallas_call(
        kernel,
        out_shape=(line, block, jax.ShapeDtypeStruct((1, LANES), jnp.float32)),
        in_specs=[hbm] * 6,
        out_specs=(hbm,) * 3,
        scratch_shapes=[
            pltpu.VMEM((1, ROWS), jnp.float32),
            pltpu.VMEM((ROWS, DIM), jnp.float32),
            pltpu.VMEM((ROWS, DIM), jnp.bfloat16),
            pltpu.VMEM((1, DIM), jnp.float32),
            pltpu.VMEM((1, ROWS), jnp.float32),
            pltpu.VMEM((ROWS, DIM), jnp.float32),
            pltpu.VMEM((1, ROWS), jnp.float32),
            pltpu.VMEM((ROWS, DIM), jnp.float32),
            pltpu.VMEM((16, BLOCK, LANES), jnp.bfloat16),
            pltpu.VMEM((8, X_ROWS, LANES), jnp.bfloat16),
            pltpu.VMEM((4, 2 * ROWS, LANES), jnp.float32),
            pltpu.VMEM((4, 2 * ROWS, DIM), jnp.float32),
            pltpu.VMEM((4, 2 * ROWS, LANES), jnp.float32),
            pltpu.VMEM((8, X_ROWS, LANES), jnp.bfloat16),
            pltpu.VMEM((8, 1, 2 * LANES), jnp.float32),
            pltpu.VMEM((8, X_ROWS, LANES), jnp.bfloat16),
            pltpu.VMEM((8, 1, 2 * LANES), jnp.float32),
            pltpu.VMEM((16, LANES), jnp.float32),
            pltpu.VMEM((1, LANES), jnp.float32),
            pltpu.VMEM((COUNT, 1, LANES), jnp.float32),
            dma((39,)),
            dma((39,)),
            dma((8,)),
            dma((8,)),
            dma((8,)),
            dma((8,)),
            dma((8,)),
            dma((8,)),
            dma,
            dma,
            dma((6,)),
        ],
        compiler_params=pltpu.CompilerParams(
            collective_id=0, has_side_effects=True, vmem_limit_bytes=GRANT
        ),
        cost_estimate=pl.CostEstimate(
            flops=9_700_000_000, bytes_accessed=2_000_000, transcendentals=4_800_000
        ),
    )(
        points,
        lengthscale.reshape(1, DIM),
        rv.reshape(1, ROWS),
        rg,
        dv.reshape(1, ROWS),
        dg,
    )
    nsv, nsg, nrv, nrg, ndv, ndg = pl.pallas_call(
        update,
        out_shape=(line, block) * 3,
        in_specs=[hbm] * 9,
        out_specs=(hbm,) * 6,
        scratch_shapes=[pltpu.VMEM((1, ROWS), jnp.float32), pltpu.VMEM((ROWS, DIM), jnp.float32)] * 7
        + [pltpu.VMEM((1, LANES), jnp.float32), dma((9,)), dma((6,))],
        compiler_params=pltpu.CompilerParams(vmem_limit_bytes=GRANT),
    )(
        sv.reshape(1, ROWS),
        sg,
        rv.reshape(1, ROWS),
        rg,
        dv.reshape(1, ROWS),
        dg,
        image_vals,
        image_grads,
        steps,
    )
    return (nsv.reshape(ROWS), nsg, nrv.reshape(ROWS), nrg, ndv.reshape(ROWS), ndg)


def solution(mesh):
    lines, blocks = P(("row", "col")), P(("row", "col"), None)
    return jax.shard_map(
        body,
        mesh=mesh,
        in_specs=(blocks, P(), lines, blocks, lines, blocks, lines, blocks),
        out_specs=(lines, blocks) * 3,
        check_vma=False,
    )
```
